32 devices in a mesh: dp: 4 (over y, core), own: 8 (over z, x).
Axes of the slice: x: 2, y: 2, z: 4, core: 2. Of those that a mesh axis runs over, the one named last changes fastest.
Arguments:
- grads: bfloat16 [4, 16, 768, 768], P('dp', 'own'), may hold values from -0.059814453 to 0.059814453
- owner: int32 [16], replicated, may hold values from 0 to 7, as said below
- weights: float32 [32, 768, 768], P('own', 'dp'), may hold values from -6 to 6
- stat_left: float32 [32, 768, 768], P('own', 'dp'), may hold values from -3 to 3
- stat_right: float32 [32, 768, 768], P('own', 'dp'), may hold values from -3 to 3
- adam_second: float32 [32, 768, 768], P('own', 'dp'), may hold values from 0.0002 to 1
- root_left: bfloat16 [32, 768, 768], P('own', 'dp'), may hold values from -0.21875 to 0.21875
- root_right: bfloat16 [32, 768, 768], P('own', 'dp'), may hold values from -0.21875 to 0.21875
Outputs:
- new_weights: bfloat16 [32, 768, 768], P('own')
- new_left: float32 [32, 768, 768], P('own', 'dp')
- new_right: float32 [32, 768, 768], P('own', 'dp')
- new_second: float32 [32, 768, 768], P('own', 'dp')
The draws below stay inside these ranges and needn't reach their ends.
Inputs may be any that keep to these rules, and one draw needn't show every extreme that they name: The 2 blocks 2 * j to 2 * j + 1 have different owners, for every j; one owner holds exactly 4 blocks and none holds more.
All inputs are finite; a program needn't handle non-finite values.
Results may differ from the reference program's by a relative error of at most 0.0095.
Values may be sent and summed in bfloat16 or wider, within the bound.
A program may use at most 64 MiB of HBM per device.

```python
import math
import jax
import jax.numpy as jnp
from jax import lax

D = 768
BLOCK = 768
BPD = 2
NB = 16
CAP = 4
SLOTS = 32
N_DP = 4
N_OWN = 8


def draw_owner(key, part):
    key_start = jax.random.fold_in(key, 11)
    key_hot = jax.random.fold_in(key, 12)
    key_rows = jax.random.fold_in(key, 13)
    key_cols = jax.random.fold_in(key, 14)
    key_order = jax.random.fold_in(key, 15)
    start = jax.random.permutation(key_start, N_OWN).astype(jnp.int32)
    base = (start[:, None] + jnp.arange(BPD, dtype=jnp.int32)[None, :]) % N_OWN
    hot = jax.random.randint(key_hot, (), 0, N_OWN).astype(jnp.int32)
    present = jnp.any(base == hot, axis=1)
    score = jax.random.randint(key_rows, (N_OWN,), 0, 1 << 20).astype(jnp.int32) * N_OWN + jax.random.permutation(key_order, N_OWN).astype(jnp.int32)
    score = jnp.where(present, -1, score)
    picked_values, picked = lax.top_k(score, BPD)
    chosen = jnp.zeros((N_OWN,), jnp.int32).at[picked].set(1) > 0
    column = jax.random.randint(key_cols, (N_OWN,), 0, BPD).astype(jnp.int32)
    replace = chosen[:, None] & (jnp.arange(BPD, dtype=jnp.int32)[None, :] == column[:, None])
    result = jnp.where(replace, hot, base)
    return result.reshape(-1).astype(jnp.int32)


def draw_adam_second(key, part):
    key_slot = jax.random.fold_in(key, 21)
    key_col = jax.random.fold_in(key, 22)
    key_noise = jax.random.fold_in(key, 23)
    slot_factor = jnp.exp(jax.random.uniform(key_slot, (SLOTS, 1, 1), jnp.float32, math.log(0.3), math.log(3.0)))
    row_factor = (10.0 ** (jnp.arange(BLOCK, dtype=jnp.float32) / (BLOCK - 1)))[None, :, None]
    col_factor = jnp.exp(jax.random.uniform(key_col, (1, 1, D), jnp.float32, 0.0, math.log(3.0)))
    noise = jax.random.uniform(key_noise, (SLOTS, BLOCK, D), jnp.float32, 0.5, 2.0)
    return (0.0016 * slot_factor * row_factor * col_factor * noise).astype(jnp.float32)


def spiked(values, key, source, target, blocks, factor):
    def block_of(position):
        return (jnp.arange(values.shape[position]) // (values.shape[position] // blocks)).reshape((-1,) + (1,) * (values.ndim - 1 - position))

    first = jax.random.permutation(key, blocks)[block_of(target)]
    second = (block_of(target) + blocks // 2) % blocks
    return jnp.where((block_of(source) == first) | (block_of(source) == second), factor * values, values)


def steps_of(stream_key, extent, shards, low, top_value):
    def one(axis_at, blocks):
        heights = jax.random.uniform(jax.random.fold_in(jax.random.fold_in(stream_key, 6), axis_at), (blocks,), jnp.float32, low / len(shards), top_value / len(shards))
        return jnp.repeat(jnp.exp(heights), extent[axis_at] // blocks).reshape((-1,) + (1,) * (len(extent) - axis_at - 1))

    factor_of = one(*shards[0])
    for cut in shards[1:]:
        factor_of = factor_of * one(*cut)
    return factor_of


def gaussian(stream_key, shape, scale, bound, cuts=(), held_as=jnp.bfloat16):
    drawn = scale * jax.random.normal(stream_key, shape, jnp.float32)
    if cuts:
        drawn = drawn * steps_of(stream_key, shape, cuts, -0.22, 0.18)
    return jnp.clip(drawn, -bound, bound).astype(held_as)


def gaussian_with(rng, extent, scale, limit, shards, heavy, held_as=jnp.bfloat16):
    drawn = scale * jax.random.normal(rng, extent, jnp.float32)
    if shards:
        drawn = drawn * steps_of(rng, extent, shards, -0.22, 0.18)
    return jnp.clip(spiked(drawn, jax.random.fold_in(rng, 3), *heavy), -limit, limit).astype(held_as)


def setup_inputs(seed: int = 0) -> dict:
    arg_keys = jax.random.split(jax.random.key(seed), 9)
    grads = gaussian_with(arg_keys[0], (N_DP, NB, BLOCK, D), 0.01, 0.059814453, ((0, 4), (1, 8)), (0, 2, 4, 2.0))
    owner = draw_owner(jax.random.fold_in(arg_keys[8], 71), 0)
    weights = gaussian(arg_keys[2], (SLOTS, BLOCK, D), 1.0, 6.0, ((0, 8), (1, 4)), jnp.float32)
    stat_left = gaussian(arg_keys[3], (SLOTS, BLOCK, BLOCK), 0.5, 3.0, ((0, 8), (1, 4)), jnp.float32)
    stat_right = gaussian(arg_keys[4], (SLOTS, D, D), 0.5, 3.0, ((0, 8), (1, 4)), jnp.float32)
    adam_second = draw_adam_second(jax.random.fold_in(arg_keys[8], 71), 0)
    root_left = gaussian(arg_keys[6], (SLOTS, BLOCK, BLOCK), BLOCK ** -0.5, 0.21875, ((0, 8), (1, 4)))
    root_right = gaussian(arg_keys[7], (SLOTS, D, D), D ** -0.5, 0.21875, ((0, 8), (1, 4)))
    return dict(grads=grads, owner=owner, weights=weights, stat_left=stat_left, stat_right=stat_right, adam_second=adam_second, root_left=root_left, root_right=root_right)


def slot_index(owner):
    count = owner.shape[0]
    same = owner[:, None] == owner[None, :]
    earlier = jnp.arange(count, dtype=jnp.int32)[None, :] < jnp.arange(count, dtype=jnp.int32)[:, None]
    rank = lax.optimization_barrier(jnp.sum((same & earlier).astype(jnp.int32), axis=1)).astype(jnp.int32)
    return (owner * CAP + rank).astype(jnp.int32)

def reference(grads, owner, weights, stat_left, stat_right, adam_second, root_left, root_right):
    total = lax.optimization_barrier(jnp.sum(grads.astype(jnp.float32), axis=0)).astype(jnp.bfloat16)
    slot = slot_index(owner)
    slot_grad = jnp.zeros((SLOTS, BLOCK, D), jnp.bfloat16).at[slot].set(total)
    grad32 = slot_grad.astype(jnp.float32)
    new_left = 0.5 * stat_left + 0.5 * jnp.einsum('sij,skj->sik', grad32, grad32)
    new_right = 0.5 * stat_right + 0.5 * jnp.einsum('sji,sjk->sik', grad32, grad32)
    new_second = 0.9 * adam_second + 0.1 * grad32 * grad32
    adam_dir = grad32 / (jnp.sqrt(new_second) + 1e-08)
    half = jnp.einsum('sij,sjk->sik', root_left.astype(jnp.float32), grad32).astype(jnp.bfloat16)
    precond = jnp.einsum('sij,sjk->sik', half.astype(jnp.float32), root_right.astype(jnp.float32))
    adam_norm = jnp.sqrt(lax.optimization_barrier(jnp.sum(adam_dir * adam_dir, axis=(1, 2))))
    prec_norm = jnp.sqrt(lax.optimization_barrier(jnp.sum(precond * precond, axis=(1, 2))))
    graft = adam_norm / (prec_norm + 1e-06)
    new_weights = (weights - graft[:, None, None] * precond).astype(jnp.bfloat16)
    return (new_weights, new_left, new_right, new_second)
```

```python
import functools

import jax
import jax.numpy as jnp
from jax import lax
from jax.experimental import pallas as pl
from jax.experimental.pallas import tpu as pltpu
from jax.sharding import PartitionSpec as P

MESH = pl.DeviceIdType.MESH
PAIR = 2


def dot(a, b):
    return lax.dot_general(a, b, (((1,), (0,)), ((), ())), preferred_element_type=jnp.float32)


def dot_nt(a, b):
    return lax.dot_general(a, b, (((1,), (1,)), ((), ())), preferred_element_type=jnp.float32)


def kernel(
    replicas,
    owners,
    owner_ref,
    grads,
    weights,
    stat_left,
    stat_right,
    adam_second,
    root_left,
    root_right,
    out_weights,
    out_left,
    out_right,
    out_second,
    own_rows,
    core_in,
    part_out,
    part_in,
    blocks,
    cross_out,
    cross_in,
    full,
    roots,
    left_v,
    right_v,
    second_v,
    weights_v,
    root_v,
    precond,
    fresh,
    norm_out,
    norm_in,
    load_sem,
    own_sem,
    store_sem,
    core_s,
    core_r,
    part_s,
    part_r,
    up_s,
    down_s,
    block_r,
    cross_s,
    cross_r,
    grad_sems,
    root_sems,
    weight_sems,
    norm_s,
    norm_r,
):
    outer = replicas // PAIR
    layers = owners // PAIR
    per_index = grads.shape[1]
    count = per_index * owners
    capacity = weights.shape[0]
    rows = weights.shape[1]
    me = lax.axis_index("dp")
    mine = lax.axis_index("own")
    y, c = lax.div(me, PAIR), lax.rem(me, PAIR)
    o, i = lax.div(mine, PAIR), lax.rem(mine, PAIR)
    f32, bf16 = jnp.float32, jnp.bfloat16

    def replica(yy, cc):
        return {"dp": yy * PAIR + cc, "own": mine}

    def group(oo, ii):
        return {"dp": me, "own": oo * PAIR + ii}

    def span(yy, cc):
        return pl.ds(pl.multiple_of((yy * PAIR + cc) * rows, rows), rows)

    def shifted(k):
        return lax.rem(y + k, outer)

    def back(k):
        return lax.rem(y + outer - k, outer)

    def remote(src, dst, send, recv, device):
        return pltpu.make_async_remote_copy(
            src_ref=src,
            dst_ref=dst,
            send_sem=send,
            recv_sem=recv,
            device_id=device,
            device_id_type=MESH,
        )

    core_peer = replica(y, 1 - c)
    cross_peer = group(o, 1 - i)
    above, below = o + 1 < layers, o >= 1

    own_copies = {}
    for b in range(per_index):
        for k in range(outer):
            copy = pltpu.make_async_copy(
                grads.at[0, b, span(shifted(k), c)], own_rows.at[b, k], own_sem.at[b, k]
            )
            copy.start()
            own_copies[b, k] = copy

    barrier = pltpu.get_barrier_semaphore()
    for k in range(1, replicas):
        pl.semaphore_signal(
            barrier,
            inc=1,
            device_id={"dp": lax.rem(me + k, replicas), "own": mine},
            device_id_type=MESH,
        )
    pl.semaphore_signal(barrier, inc=1, device_id=cross_peer, device_id_type=MESH)

    @pl.when(above)
    def _():
        pl.semaphore_signal(barrier, inc=1, device_id=group(o + 1, i), device_id_type=MESH)

    @pl.when(below)
    def _():
        pl.semaphore_signal(barrier, inc=1, device_id=group(o - 1, i), device_id_type=MESH)

    lines = above.astype(jnp.int32) + below.astype(jnp.int32)
    pl.semaphore_wait(barrier, replicas + lines)

    order = list(range(1, outer)) + [0]
    core_copies = {}
    for b in range(per_index):
        for k in order:
            copy = remote(
                grads.at[0, b, span(shifted(k), 1 - c)],
                core_in.at[b, k],
                core_s.at[b, k],
                core_r.at[b, k],
                core_peer,
            )
            copy.start()
            core_copies[b, k] = copy

    loads = [
        pltpu.make_async_copy(root_right, roots.at[:, span(y, c)], load_sem.at[0]),
        pltpu.make_async_copy(adam_second, second_v, load_sem.at[1]),
        pltpu.make_async_copy(root_left, root_v, load_sem.at[2]),
        pltpu.make_async_copy(weights, weights_v, load_sem.at[3]),
        pltpu.make_async_copy(stat_left, left_v, load_sem.at[4]),
        pltpu.make_async_copy(stat_right, right_v, load_sem.at[5]),
    ]
    for copy in loads:
        copy.start()

    part_copies = []
    for b in range(per_index):
        for k in range(1, outer):
            own_copies[b, k].wait()
            core_copies[b, k].wait_recv()
            part_out[b, k - 1] = (
                own_rows[b, k].astype(f32) + core_in[b, k].astype(f32)
            ).astype(bf16)
            copy = remote(
                part_out.at[b, k - 1],
                part_in.at[b, k - 1],
                part_s.at[b, k - 1],
                part_r.at[b, k - 1],
                replica(shifted(k), c),
            )
            copy.start()
            part_copies.append(copy)

    def far_copy(src, ref, s, k, sems):
        return remote(
            src, ref.at[s, span(y, c)], sems.at[0, s, k], sems.at[1, s, k], replica(shifted(k), c)
        )

    def near_copy(src, ref, s, k, sems):
        return remote(
            src, ref.at[s, span(back(k), c)], sems.at[2, s, k], sems.at[3, s, k], core_peer
        )

    def gather_start(src, ref, s, sems):
        for k in range(1, outer):
            far_copy(src, ref, s, k, sems).start()
        near_copy(src, ref, s, 0, sems).start()

    def gather_forward(ref, s, sems):
        for k in range(1, outer):
            landed = ref.at[s, span(back(k), c)]
            remote(landed, landed, sems.at[0, s, k], sems.at[1, s, k], core_peer).wait_recv()
            near_copy(landed, ref, s, k, sems).start()

    def gather_arrived(ref, s, sems):
        for k in range(outer):
            landed = ref.at[s, span(back(k), 1 - c)]
            remote(landed, landed, sems.at[2, s, k], sems.at[3, s, k], core_peer).wait_recv()

    def gather_sent(src, ref, s, sems):
        for k in range(1, outer):
            far_copy(src, ref, s, k, sems).wait_send()
        for k in range(outer):
            near_copy(src, ref, s, k, sems).wait_send()

    def slots(body):
        def step(s, carry):
            body(s)
            return carry

        lax.fori_loop(0, capacity, step, 0)

    loads[0].wait()
    slots(lambda s: gather_start(roots.at[s, span(y, c)], roots, s, root_sems))

    def send_up(src, k, b):
        return remote(
            blocks.at[src, b],
            blocks.at[src, b],
            up_s.at[k, b],
            block_r.at[src, b],
            group(o + 1, i),
        )

    def send_down(src, k, b):
        return remote(
            blocks.at[src, b],
            blocks.at[src, b],
            down_s.at[k, b],
            block_r.at[src, b],
            group(o - 1, i),
        )

    def wait_block(src, b):
        remote(
            blocks.at[src, b], blocks.at[src, b], up_s.at[0, b], block_r.at[src, b], cross_peer
        ).wait_recv()

    def cross_copy(src):
        return remote(
            cross_out.at[src], cross_in.at[src], cross_s.at[src], cross_r.at[src], cross_peer
        )

    def cross(src):
        first = (src * PAIR + i) * per_index
        other = o * PAIR + 1 - i
        sent = blocks[src, 0]
        for b in range(1, per_index):
            sent = jnp.where(owner_ref[first + b] == other, blocks[src, b], sent)
        cross_out[src] = sent
        cross_copy(src).start()

    for b in range(per_index):
        own_copies[b, 0].wait()
        core_copies[b, 0].wait_recv()
        total = own_rows[b, 0].astype(f32) + core_in[b, 0].astype(f32)
        for k in range(1, outer):
            remote(
                part_out.at[b, k - 1],
                part_in.at[b, k - 1],
                part_s.at[b, k - 1],
                part_r.at[b, k - 1],
                core_peer,
            ).wait_recv()
            total = total + part_in[b, k - 1].astype(f32)
        blocks[o, b] = total.astype(bf16)

        @pl.when(above)
        def _():
            send_up(o, 0, b).start()

        @pl.when(below)
        def _():
            send_down(o, 0, b).start()

    cross(o)
    for d in range(1, layers):
        for b in range(per_index):

            @pl.when(o >= d)
            def _():
                wait_block(o - d, b)

                @pl.when(above)
                def _():
                    send_up(o - d, d, b).start()

            @pl.when(o + d < layers)
            def _():
                wait_block(o + d, b)

                @pl.when(below)
                def _():
                    send_down(o + d, d, b).start()

        @pl.when(o >= d)
        def _():
            cross(o - d)

        @pl.when(o + d < layers)
        def _():
            cross(o + d)

    slots(lambda s: gather_forward(roots, s, root_sems))
    for src in range(layers):
        cross_copy(src).wait_recv()

    def choose(s):
        found = jnp.int32(0)
        seen = jnp.int32(0)
        valid = jnp.int32(0)
        for b in range(count):
            hit = (owner_ref[b] == mine).astype(jnp.int32)
            take = hit * (seen == s).astype(jnp.int32)
            found = found + take * b
            valid = valid + take
            seen = seen + hit
        source = lax.div(found, per_index)
        layer, side = lax.div(source, PAIR), lax.rem(source, PAIR)
        straight = blocks[layer, lax.rem(found, per_index)]
        crossed = cross_in[layer]
        picked = jnp.where(side == i, straight, crossed)
        full[s, span(y, c)] = jnp.where(valid == 1, picked, jnp.zeros_like(picked))
        gather_start(full.at[s, span(y, c)], full, s, grad_sems)

    slots(choose)
    for copy in loads[1:]:
        copy.wait()

    def store(ref, out, which, s):
        return pltpu.make_async_copy(ref.at[s], out.at[s], store_sem.at[which, s])

    row_of = lax.broadcasted_iota(jnp.int32, (8, 128), 0)

    def norm_copy(s, k):
        return remote(
            norm_out.at[s],
            norm_in.at[k - 1, s],
            norm_s.at[s, k - 1],
            norm_r.at[s, k - 1],
            {"dp": lax.rem(me + k, replicas), "own": mine},
        )

    def own_output(s):
        return pltpu.make_async_copy(
            fresh.at[s], out_weights.at[s, span(y, c)], store_sem.at[3, s]
        )

    def update(s):
        norms = norm_out[s]
        for k in range(1, replicas):
            norm_copy(s, k).wait_recv()
            norms = norms + norm_in[k - 1, s]
        graft = jnp.sqrt(norms[0:1, 0:1]) / (jnp.sqrt(norms[4:5, 0:1]) + 1e-06)
        fresh[s] = (weights_v[s] - graft * precond[s]).astype(bf16)
        gather_start(fresh.at[s], out_weights, s, weight_sems)
        own_output(s).start()

    def precondition(s):
        grad32 = full[s, span(y, c)].astype(f32)
        second = 0.9 * second_v[s] + 0.1 * grad32 * grad32
        second_v[s] = second
        store(second_v, out_second, 0, s).start()
        direction = grad32 / (jnp.sqrt(second) + 1e-08)
        adam_sq = jnp.sum(direction * direction)
        gather_forward(full, s, grad_sems)
        gather_arrived(full, s, grad_sems)
        gather_arrived(roots, s, root_sems)
        half = dot(root_v[s], full[s]).astype(bf16)
        result = dot(half, roots[s])
        precond[s] = result
        norm_out[s] = jnp.where(row_of < 4, adam_sq, jnp.sum(result * result))
        for k in range(1, replicas):
            norm_copy(s, k).start()

        @pl.when(s >= 1)
        def _():
            update(s - 1)

    slots(precondition)
    update(capacity - 1)

    width = full.shape[2]
    cols = width // replicas
    shape = (cols, width)
    pick = (
        lax.broadcasted_iota(jnp.int32, shape, 1)
        == lax.broadcasted_iota(jnp.int32, shape, 0) + me * cols
    ).astype(f32).astype(bf16)

    def statistics(s):
        left_v[s] = 0.5 * left_v[s] + 0.5 * dot_nt(full[s, span(y, c)], full[s])
        store(left_v, out_left, 1, s).start()
        columns = dot_nt(pick, full[s]).astype(bf16)
        right_v[s] = 0.5 * right_v[s] + 0.5 * dot(columns, full[s])
        store(right_v, out_right, 2, s).start()
        gather_forward(out_weights, s, weight_sems)

    slots(statistics)

    for copy in list(core_copies.values()) + part_copies:
        copy.wait_send()
    for k in range(layers - 1):
        for b in range(per_index):

            @pl.when(above & (o >= k))
            def _():
                send_up(o - k, k, b).wait_send()

            @pl.when(below & (o + k < layers))
            def _():
                send_down(o + k, k, b).wait_send()

    for src in range(layers):
        cross_copy(src).wait_send()

    def finish(s):
        gather_sent(roots.at[s, span(y, c)], roots, s, root_sems)
        gather_sent(full.at[s, span(y, c)], full, s, grad_sems)
        for k in range(1, replicas):
            norm_copy(s, k).wait_send()
        store(second_v, out_second, 0, s).wait()
        store(left_v, out_left, 1, s).wait()
        store(right_v, out_right, 2, s).wait()
        own_output(s).wait()
        gather_arrived(out_weights, s, weight_sems)
        gather_sent(fresh.at[s], out_weights, s, weight_sems)

    slots(finish)


def on_device(
    replicas,
    owners,
    grads,
    owner,
    weights,
    stat_left,
    stat_right,
    adam_second,
    root_left,
    root_right,
):
    capacity, rows, width = weights.shape
    per_index, height = grads.shape[1], grads.shape[2]
    outer, layers = replicas // PAIR, owners // PAIR
    bf16, f32 = jnp.bfloat16, jnp.float32
    block = (rows, width)
    several = max(outer - 1, 1)
    dma = pltpu.SemaphoreType.DMA
    anywhere = pl.BlockSpec(memory_space=pl.ANY)
    scratch = [
        pltpu.VMEM((per_index, outer) + block, bf16),
        pltpu.VMEM((per_index, outer) + block, bf16),
        pltpu.VMEM((per_index, several) + block, bf16),
        pltpu.VMEM((per_index, several) + block, bf16),
        pltpu.VMEM((layers, per_index) + block, bf16),
        pltpu.VMEM((layers,) + block, bf16),
        pltpu.VMEM((layers,) + block, bf16),
        pltpu.VMEM((capacity, height, width), bf16),
        pltpu.VMEM((capacity, width, width), bf16),
        pltpu.VMEM(stat_left.shape, f32),
        pltpu.VMEM(stat_right.shape, f32),
        pltpu.VMEM(adam_second.shape, f32),
        pltpu.VMEM(weights.shape, f32),
        pltpu.VMEM(root_left.shape, bf16),
        pltpu.VMEM(weights.shape, f32),
        pltpu.VMEM(weights.shape, bf16),
        pltpu.VMEM((capacity, 8, 128), f32),
        pltpu.VMEM((replicas - 1, capacity, 8, 128), f32),
        dma((6,)),
        dma((per_index, outer)),
        dma((4, capacity)),
        dma((per_index, outer)),
        dma((per_index, outer)),
        dma((per_index, several)),
        dma((per_index, several)),
        dma((layers, per_index)),
        dma((layers, per_index)),
        dma((layers, per_index)),
        dma((layers,)),
        dma((layers,)),
        dma((4, capacity, outer)),
        dma((4, capacity, outer)),
        dma((4, capacity, outer)),
        dma((capacity, replicas - 1)),
        dma((capacity, replicas - 1)),
    ]
    products = 5 * 2 * capacity * rows * width * width
    moved = 2 * grads.size + 32 * weights.size + 2 * capacity * height * width
    return pl.pallas_call(
        functools.partial(kernel, replicas, owners),
        out_shape=(
            jax.ShapeDtypeStruct((capacity, height, width), bf16),
            jax.ShapeDtypeStruct(stat_left.shape, f32),
            jax.ShapeDtypeStruct(stat_right.shape, f32),
            jax.ShapeDtypeStruct(adam_second.shape, f32),
        ),
        in_specs=[pl.BlockSpec(memory_space=pltpu.SMEM)] + [anywhere] * 7,
        out_specs=(anywhere,) * 4,
        scratch_shapes=scratch,
        cost_estimate=pl.CostEstimate(
            flops=products, bytes_accessed=moved, transcendentals=weights.size
        ),
        compiler_params=pltpu.CompilerParams(
            collective_id=0, has_side_effects=True, vmem_limit_bytes=56 * 1024 * 1024
        ),
    )(owner, grads, weights, stat_left, stat_right, adam_second, root_left, root_right)


def solution(mesh):
    placed = (
        P("dp", "own", None, None),
        P(),
        P("own", "dp", None),
        P("own", "dp", None),
        P("own", "dp", None),
        P("own", "dp", None),
        P("own", "dp", None),
        P("own", "dp", None),
    )
    return jax.shard_map(
        functools.partial(on_device, mesh.shape["dp"], mesh.shape["own"]),
        mesh=mesh,
        in_specs=placed,
        out_specs=(
            P("own", None, None),
            P("own", "dp", None),
            P("own", "dp", None),
            P("own", "dp", None),
        ),
        check_vma=False,
    )
```

```python
import functools

import jax
import jax.numpy as jnp
from jax import lax
from jax.experimental import pallas as pl
from jax.experimental.pallas import tpu as pltpu
from jax.sharding import PartitionSpec as P

MESH = pl.DeviceIdType.MESH
PAIR = 2
CHUNK = 256


def dot(a, b):
    return lax.dot_general(a, b, (((1,), (0,)), ((), ())), preferred_element_type=jnp.float32)


def dot_nt(a, b):
    return lax.dot_general(a, b, (((1,), (1,)), ((), ())), preferred_element_type=jnp.float32)


def kernel(
    replicas,
    owners,
    owner_ref,
    grads,
    weights,
    stat_left,
    stat_right,
    adam_second,
    root_left,
    root_right,
    out_weights,
    out_left,
    out_right,
    out_second,
    own_rows,
    core_in,
    part_out,
    part_in,
    blocks,
    cross_out,
    cross_in,
    full,
    roots,
    left_v,
    right_v,
    second_v,
    weights_v,
    root_v,
    precond,
    fresh,
    norm_out,
    norm_in,
    load_sem,
    own_sem,
    store_sem,
    core_s,
    core_r,
    part_s,
    part_r,
    up_s,
    down_s,
    block_r,
    cross_s,
    cross_r,
    grad_sems,
    root_sems,
    weight_sems,
    norm_s,
    norm_r,
):
    outer = replicas // PAIR
    layers = owners // PAIR
    per_index = grads.shape[1]
    count = per_index * owners
    capacity = weights.shape[0]
    rows = weights.shape[1]
    chunks = weights.shape[2] // CHUNK
    me = lax.axis_index("dp")
    mine = lax.axis_index("own")
    y, c = lax.div(me, PAIR), lax.rem(me, PAIR)
    o, i = lax.div(mine, PAIR), lax.rem(mine, PAIR)
    f32, bf16 = jnp.float32, jnp.bfloat16

    def replica(yy, cc):
        return {"dp": yy * PAIR + cc, "own": mine}

    def group(oo, ii):
        return {"dp": me, "own": oo * PAIR + ii}

    def span(yy, cc):
        return pl.ds(pl.multiple_of((yy * PAIR + cc) * rows, rows), rows)

    def part(q):
        return pl.ds(q * CHUNK, CHUNK)

    def shifted(k):
        return lax.rem(y + k, outer)

    def back(k):
        return lax.rem(y + outer - k, outer)

    def remote(src, dst, send, recv, device):
        return pltpu.make_async_remote_copy(
            src_ref=src,
            dst_ref=dst,
            send_sem=send,
            recv_sem=recv,
            device_id=device,
            device_id_type=MESH,
        )

    core_peer = replica(y, 1 - c)
    cross_peer = group(o, 1 - i)
    above, below = o + 1 < layers, o >= 1

    own_copies = {}
    for b in range(per_index):
        for k in range(outer):
            copy = pltpu.make_async_copy(
                grads.at[0, b, span(shifted(k), c)], own_rows.at[k, b], own_sem.at[b, k]
            )
            copy.start()
            own_copies[b, k] = copy

    barrier = pltpu.get_barrier_semaphore()
    for k in range(1, replicas):
        pl.semaphore_signal(
            barrier,
            inc=1,
            device_id={"dp": lax.rem(me + k, replicas), "own": mine},
            device_id_type=MESH,
        )
    pl.semaphore_signal(barrier, inc=1, device_id=cross_peer, device_id_type=MESH)

    @pl.when(above)
    def _():
        pl.semaphore_signal(barrier, inc=1, device_id=group(o + 1, i), device_id_type=MESH)

    @pl.when(below)
    def _():
        pl.semaphore_signal(barrier, inc=1, device_id=group(o - 1, i), device_id_type=MESH)

    lines = above.astype(jnp.int32) + below.astype(jnp.int32)
    pl.semaphore_wait(barrier, replicas + lines)

    order = list(range(1, outer)) + [0]
    core_copies = {}
    for k in order:
        for b in range(per_index):
            copy = remote(
                grads.at[0, b, span(shifted(k), 1 - c)],
                core_in.at[k, b],
                core_s.at[b, k],
                core_r.at[b, k],
                core_peer,
            )
            copy.start()
            core_copies[b, k] = copy

    loads = [
        pltpu.make_async_copy(root_right, roots.at[:, span(y, c)], load_sem.at[0]),
        pltpu.make_async_copy(adam_second, second_v, load_sem.at[1]),
        pltpu.make_async_copy(root_left, root_v, load_sem.at[2]),
        pltpu.make_async_copy(weights, weights_v, load_sem.at[3]),
        pltpu.make_async_copy(stat_left, left_v, load_sem.at[4]),
        pltpu.make_async_copy(stat_right, right_v, load_sem.at[5]),
    ]
    for copy in loads:
        copy.start()

    def part_copy(q, k):
        return remote(
            part_out.at[q, k - 1],
            part_in.at[q, k - 1],
            part_s.at[q, k - 1],
            part_r.at[q, k - 1],
            replica(shifted(k), c),
        )

    def chip_sum(q, k):
        return own_rows[k, :, :, part(q)].astype(f32) + core_in[k, :, :, part(q)].astype(f32)

    for q in range(chunks):
        for k in range(1, outer):
            if q == 0:
                for b in range(per_index):
                    own_copies[b, k].wait()
                    core_copies[b, k].wait_recv()
            part_out[q, k - 1] = chip_sum(q, k).astype(bf16)
            part_copy(q, k).start()

    def far_copy(src, ref, s, k, sems):
        return remote(
            src, ref.at[s, span(y, c)], sems.at[0, s, k], sems.at[1, s, k], replica(shifted(k), c)
        )

    def near_copy(src, ref, s, k, sems):
        return remote(
            src, ref.at[s, span(back(k), c)], sems.at[2, s, k], sems.at[3, s, k], core_peer
        )

    def gather_start(src, ref, s, sems):
        for k in range(1, outer):
            far_copy(src, ref, s, k, sems).start()
        near_copy(src, ref, s, 0, sems).start()

    def gather_forward(ref, s, sems):
        for k in range(1, outer):
            landed = ref.at[s, span(back(k), c)]
            remote(landed, landed, sems.at[0, s, k], sems.at[1, s, k], core_peer).wait_recv()
            near_copy(landed, ref, s, k, sems).start()

    def gather_arrived(ref, s, sems):
        for k in range(outer):
            landed = ref.at[s, span(back(k), 1 - c)]
            remote(landed, landed, sems.at[2, s, k], sems.at[3, s, k], core_peer).wait_recv()

    def gather_sent(src, ref, s, sems):
        for k in range(1, outer):
            far_copy(src, ref, s, k, sems).wait_send()
        for k in range(outer):
            near_copy(src, ref, s, k, sems).wait_send()

    def slots(body):
        def step(s, carry):
            body(s)
            return carry

        lax.fori_loop(0, capacity, step, 0)

    loads[0].wait()
    slots(lambda s: gather_start(roots.at[s, span(y, c)], roots, s, root_sems))

    def send_up(src, d, q):
        return remote(
            blocks.at[src, q],
            blocks.at[src, q],
            up_s.at[d, q],
            block_r.at[src, q],
            group(o + 1, i),
        )

    def send_down(src, d, q):
        return remote(
            blocks.at[src, q],
            blocks.at[src, q],
            down_s.at[d, q],
            block_r.at[src, q],
            group(o - 1, i),
        )

    def wait_block(src, q):
        remote(
            blocks.at[src, q], blocks.at[src, q], up_s.at[0, q], block_r.at[src, q], cross_peer
        ).wait_recv()

    def cross_copy(src, q):
        return remote(
            cross_out.at[src, q],
            cross_in.at[src, q],
            cross_s.at[src, q],
            cross_r.at[src, q],
            cross_peer,
        )

    def cross(src, q):
        first = (src * PAIR + i) * per_index
        other = o * PAIR + 1 - i
        sent = blocks[src, q, 0]
        for b in range(1, per_index):
            sent = jnp.where(owner_ref[first + b] == other, blocks[src, q, b], sent)
        cross_out[src, q] = sent
        cross_copy(src, q).start()

    def own_total(q):
        if q == 0:
            for b in range(per_index):
                own_copies[b, 0].wait()
                core_copies[b, 0].wait_recv()
        total = chip_sum(q, 0)
        for k in range(1, outer):
            part_copy(q, k).wait_recv()
            total = total + part_in[q, k - 1].astype(f32)
        blocks[o, q] = total.astype(bf16)

        @pl.when(above)
        def _():
            send_up(o, 0, q).start()

        @pl.when(below)
        def _():
            send_down(o, 0, q).start()

        cross(o, q)

    def pass_on(d, q):
        @pl.when(o >= d)
        def _():
            wait_block(o - d, q)

            @pl.when(above)
            def _():
                send_up(o - d, d, q).start()

        @pl.when(o + d < layers)
        def _():
            wait_block(o + d, q)

            @pl.when(below)
            def _():
                send_down(o + d, d, q).start()

        @pl.when(o >= d)
        def _():
            cross(o - d, q)

        @pl.when(o + d < layers)
        def _():
            cross(o + d, q)

    def choose(q, s):
        found = jnp.int32(0)
        seen = jnp.int32(0)
        valid = jnp.int32(0)
        for b in range(count):
            hit = (owner_ref[b] == mine).astype(jnp.int32)
            take = hit * (seen == s).astype(jnp.int32)
            found = found + take * b
            valid = valid + take
            seen = seen + hit
        source = lax.div(found, per_index)
        layer, side = lax.div(source, PAIR), lax.rem(source, PAIR)
        within = lax.rem(found, per_index)
        crossed = jnp.zeros_like(cross_in[0, q])
        for src in range(layers):
            taken = cross_in[src, q]
            for b in range(per_index):
                straight = blocks[src, q, b]
                taken = jnp.where((side == i) & (within == b), straight, taken)
            crossed = jnp.where((layer == src) & (valid == 1), taken, crossed)
        f = q * capacity + s
        full[f, span(y, c)] = crossed
        gather_start(full.at[f, span(y, c)], full, f, grad_sems)

    def choose_chunk(q):
        for src in range(layers):
            cross_copy(src, q).wait_recv()
        slots(functools.partial(choose, q))

    for t in range(chunks + layers):
        if 0 <= t - layers < chunks:
            choose_chunk(t - layers)
        for d in range(layers - 1, 0, -1):
            if 0 <= t - d < chunks:
                pass_on(d, t - d)
        if t < chunks:
            own_total(t)

    for copy in loads[1:]:
        copy.wait()

    def store(ref, out, which, s):
        return pltpu.make_async_copy(ref.at[s], out.at[s], store_sem.at[which, s])

    row_of = lax.broadcasted_iota(jnp.int32, (8, 128), 0)

    def norm_copy(s, k):
        return remote(
            norm_out.at[s],
            norm_in.at[k - 1, s],
            norm_s.at[s, k - 1],
            norm_r.at[s, k - 1],
            {"dp": lax.rem(me + k, replicas), "own": mine},
        )

    def own_output(s):
        return pltpu.make_async_copy(
            fresh.at[s], out_weights.at[s, span(y, c)], store_sem.at[3, s]
        )

    def moments(s):
        adam_sq = jnp.float32(0)
        for q in range(chunks):
            grad32 = full[q * capacity + s, span(y, c)].astype(f32)
            second = 0.9 * second_v[s, :, part(q)] + 0.1 * grad32 * grad32
            second_v[s, :, part(q)] = second
            direction = grad32 / (jnp.sqrt(second) + 1e-08)
            adam_sq = adam_sq + jnp.sum(direction * direction)
        norm_out[s] = jnp.where(row_of < 4, adam_sq, 0.0)
        store(second_v, out_second, 0, s).start()

    def product(q, s):
        f = q * capacity + s
        gather_arrived(full, f, grad_sems)
        half = dot(root_v[s], full[f]).astype(bf16)
        return dot(half, roots[s, part(q), :])

    def accumulate(q, s):
        if q == 0:
            gather_arrived(roots, s, root_sems)
            precond[s] = product(q, s)
        else:
            precond[s] = precond[s] + product(q, s)

    def precondition(s):
        accumulate(chunks - 1, s)
        result = precond[s]
        norm_out[s] = norm_out[s] + jnp.where(row_of < 4, 0.0, jnp.sum(result * result))
        for k in range(1, replicas):
            norm_copy(s, k).start()

    def update(s):
        norms = norm_out[s]
        for k in range(1, replicas):
            norm_copy(s, k).wait_recv()
            norms = norms + norm_in[k - 1, s]
        graft = jnp.sqrt(norms[0:1, 0:1]) / (jnp.sqrt(norms[4:5, 0:1]) + 1e-06)
        fresh[s] = (weights_v[s] - graft * precond[s]).astype(bf16)
        gather_start(fresh.at[s], out_weights, s, weight_sems)
        own_output(s).start()

    slots(moments)
    slots(lambda s: gather_forward(roots, s, root_sems))
    for q in range(chunks - 1):
        slots(lambda s: gather_forward(full, q * capacity + s, grad_sems))
        slots(functools.partial(accumulate, q))

    def last(s, carry):
        @pl.when(s < capacity)
        def _():
            gather_forward(full, (chunks - 1) * capacity + s, grad_sems)

        @pl.when((s >= 1) & (s <= capacity))
        def _():
            precondition(s - 1)

        @pl.when(s >= 2)
        def _():
            update(s - 2)

        return carry

    lax.fori_loop(0, capacity + 2, last, 0)

    width = weights.shape[2]
    cols = width // replicas

    def pick(q):
        shape = (cols, CHUNK)
        column = lax.broadcasted_iota(jnp.int32, shape, 1) + q * CHUNK
        wanted = lax.broadcasted_iota(jnp.int32, shape, 0) + me * cols
        return (column == wanted).astype(f32).astype(bf16)

    def statistics(s):
        left, columns = 0.0, 0.0
        for q in range(chunks):
            f = q * capacity + s
            left = left + dot_nt(full[f, span(y, c)], full[f])
            columns = columns + dot_nt(pick(q), full[f])
        left_v[s] = 0.5 * left_v[s] + 0.5 * left
        store(left_v, out_left, 1, s).start()
        columns = columns.astype(bf16)
        for q in range(chunks):
            right_v[s, :, part(q)] = 0.5 * right_v[s, :, part(q)] + 0.5 * dot(
                columns, full[q * capacity + s]
            )
        store(right_v, out_right, 2, s).start()
        gather_forward(out_weights, s, weight_sems)

    slots(statistics)

    for copy in core_copies.values():
        copy.wait_send()
    for q in range(chunks):
        for k in range(1, outer):
            part_copy(q, k).wait_send()
        for d in range(layers - 1):

            @pl.when(above & (o >= d))
            def _():
                send_up(o - d, d, q).wait_send()

            @pl.when(below & (o + d < layers))
            def _():
                send_down(o + d, d, q).wait_send()

        for src in range(layers):
            cross_copy(src, q).wait_send()

    def finish(s):
        gather_sent(roots.at[s, span(y, c)], roots, s, root_sems)
        for q in range(chunks):
            f = q * capacity + s
            gather_sent(full.at[f, span(y, c)], full, f, grad_sems)
        for k in range(1, replicas):
            norm_copy(s, k).wait_send()
        store(second_v, out_second, 0, s).wait()
        store(left_v, out_left, 1, s).wait()
        store(right_v, out_right, 2, s).wait()
        own_output(s).wait()
        gather_arrived(out_weights, s, weight_sems)
        gather_sent(fresh.at[s], out_weights, s, weight_sems)

    slots(finish)


def on_device(
    replicas,
    owners,
    grads,
    owner,
    weights,
    stat_left,
    stat_right,
    adam_second,
    root_left,
    root_right,
):
    capacity, rows, width = weights.shape
    per_index, height = grads.shape[1], grads.shape[2]
    outer, layers = replicas // PAIR, owners // PAIR
    bf16, f32 = jnp.bfloat16, jnp.float32
    block, piece = (rows, width), (rows, CHUNK)
    chunks = width // CHUNK
    several = max(outer - 1, 1)
    dma = pltpu.SemaphoreType.DMA
    anywhere = pl.BlockSpec(memory_space=pl.ANY)
    scratch = [
        pltpu.VMEM((outer, per_index) + block, bf16),
        pltpu.VMEM((outer, per_index) + block, bf16),
        pltpu.VMEM((chunks, several, per_index) + piece, bf16),
        pltpu.VMEM((chunks, several, per_index) + piece, bf16),
        pltpu.VMEM((layers, chunks, per_index) + piece, bf16),
        pltpu.VMEM((layers, chunks) + piece, bf16),
        pltpu.VMEM((layers, chunks) + piece, bf16),
        pltpu.VMEM((chunks * capacity, height, CHUNK), bf16),
        pltpu.VMEM((capacity, width, width), bf16),
        pltpu.VMEM(stat_left.shape, f32),
        pltpu.VMEM(stat_right.shape, f32),
        pltpu.VMEM(adam_second.shape, f32),
        pltpu.VMEM(weights.shape, f32),
        pltpu.VMEM(root_left.shape, bf16),
        pltpu.VMEM(weights.shape, f32),
        pltpu.VMEM(weights.shape, bf16),
        pltpu.VMEM((capacity, 8, 128), f32),
        pltpu.VMEM((replicas - 1, capacity, 8, 128), f32),
        dma((6,)),
        dma((per_index, outer)),
        dma((4, capacity)),
        dma((per_index, outer)),
        dma((per_index, outer)),
        dma((chunks, several)),
        dma((chunks, several)),
        dma((layers, chunks)),
        dma((layers, chunks)),
        dma((layers, chunks)),
        dma((layers, chunks)),
        dma((layers, chunks)),
        dma((4, chunks * capacity, outer)),
        dma((4, capacity, outer)),
        dma((4, capacity, outer)),
        dma((capacity, replicas - 1)),
        dma((capacity, replicas - 1)),
    ]
    products = 5 * 2 * capacity * rows * width * width
    moved = 2 * grads.size + 32 * weights.size + 2 * capacity * height * width
    return pl.pallas_call(
        functools.partial(kernel, replicas, owners),
        out_shape=(
            jax.ShapeDtypeStruct((capacity, height, width), bf16),
            jax.ShapeDtypeStruct(stat_left.shape, f32),
            jax.ShapeDtypeStruct(stat_right.shape, f32),
            jax.ShapeDtypeStruct(adam_second.shape, f32),
        ),
        in_specs=[pl.BlockSpec(memory_space=pltpu.SMEM)] + [anywhere] * 7,
        out_specs=(anywhere,) * 4,
        scratch_shapes=scratch,
        cost_estimate=pl.CostEstimate(
            flops=products, bytes_accessed=moved, transcendentals=weights.size
        ),
        compiler_params=pltpu.CompilerParams(
            collective_id=0, has_side_effects=True, vmem_limit_bytes=40 * 1024 * 1024
        ),
    )(owner, grads, weights, stat_left, stat_right, adam_second, root_left, root_right)


def solution(mesh):
    placed = (
        P("dp", "own", None, None),
        P(),
        P("own", "dp", None),
        P("own", "dp", None),
        P("own", "dp", None),
        P("own", "dp", None),
        P("own", "dp", None),
        P("own", "dp", None),
    )
    return jax.shard_map(
        functools.partial(on_device, mesh.shape["dp"], mesh.shape["own"]),
        mesh=mesh,
        in_specs=placed,
        out_specs=(
            P("own", None, None),
            P("own", "dp", None),
            P("own", "dp", None),
            P("own", "dp", None),
        ),
        check_vma=False,
    )
```

```python
import functools

import jax
import jax.numpy as jnp
from jax import lax
from jax.experimental import pallas as pl
from jax.experimental.pallas import tpu as pltpu
from jax.sharding import PartitionSpec as P

MESH = pl.DeviceIdType.MESH
PAIR = 2
CHUNK = 256


def dot(a, b):
    return lax.dot_general(a, b, (((1,), (0,)), ((), ())), preferred_element_type=jnp.float32)


def dot_nt(a, b):
    return lax.dot_general(a, b, (((1,), (1,)), ((), ())), preferred_element_type=jnp.float32)


def kernel(
    replicas,
    owners,
    owner_ref,
    grads,
    weights,
    stat_left,
    stat_right,
    adam_second,
    root_left,
    root_right,
    out_weights,
    out_left,
    out_right,
    out_second,
    own_rows,
    core_in,
    part_out,
    part_in,
    blocks,
    cross_out,
    cross_in,
    full,
    roots,
    left_v,
    right_v,
    second_v,
    weights_v,
    root_v,
    precond,
    fresh,
    norm_out,
    norm_in,
    load_sem,
    own_sem,
    store_sem,
    core_s,
    core_r,
    part_s,
    part_r,
    up_s,
    down_s,
    block_r,
    cross_s,
    cross_r,
    grad_sems,
    root_sems,
    weight_sems,
    norm_s,
    norm_r,
):
    outer = replicas // PAIR
    layers = owners // PAIR
    per_index = grads.shape[1]
    count = per_index * owners
    capacity = weights.shape[0]
    rows = weights.shape[1]
    chunks = weights.shape[2] // CHUNK
    me = lax.axis_index("dp")
    mine = lax.axis_index("own")
    y, c = lax.div(me, PAIR), lax.rem(me, PAIR)
    o, i = lax.div(mine, PAIR), lax.rem(mine, PAIR)
    f32, bf16 = jnp.float32, jnp.bfloat16

    def replica(yy, cc):
        return {"dp": yy * PAIR + cc, "own": mine}

    def group(oo, ii):
        return {"dp": me, "own": oo * PAIR + ii}

    def span(yy, cc):
        return pl.ds(pl.multiple_of((yy * PAIR + cc) * rows, rows), rows)

    def part(q):
        return pl.ds(q * CHUNK, CHUNK)

    def shifted(k):
        return lax.rem(y + k, outer)

    def back(k):
        return lax.rem(y + outer - k, outer)

    def remote(src, dst, send, recv, device):
        return pltpu.make_async_remote_copy(
            src_ref=src,
            dst_ref=dst,
            send_sem=send,
            recv_sem=recv,
            device_id=device,
            device_id_type=MESH,
        )

    core_peer = replica(y, 1 - c)
    cross_peer = group(o, 1 - i)
    above, below = o + 1 < layers, o >= 1

    own_copies = {}
    for b in range(per_index):
        for k in range(outer):
            copy = pltpu.make_async_copy(
                grads.at[0, b, span(shifted(k), c)], own_rows.at[k, b], own_sem.at[b, k]
            )
            copy.start()
            own_copies[b, k] = copy

    barrier = pltpu.get_barrier_semaphore()
    for k in range(1, replicas):
        pl.semaphore_signal(
            barrier,
            inc=1,
            device_id={"dp": lax.rem(me + k, replicas), "own": mine},
            device_id_type=MESH,
        )
    pl.semaphore_signal(barrier, inc=1, device_id=cross_peer, device_id_type=MESH)

    @pl.when(above)
    def _():
        pl.semaphore_signal(barrier, inc=1, device_id=group(o + 1, i), device_id_type=MESH)

    @pl.when(below)
    def _():
        pl.semaphore_signal(barrier, inc=1, device_id=group(o - 1, i), device_id_type=MESH)

    lines = above.astype(jnp.int32) + below.astype(jnp.int32)
    pl.semaphore_wait(barrier, replicas + lines)

    order = list(range(1, outer)) + [0]
    core_copies = {}
    for k in order:
        for b in range(per_index):
            copy = remote(
                grads.at[0, b, span(shifted(k), 1 - c)],
                core_in.at[k, b],
                core_s.at[b, k],
                core_r.at[b, k],
                core_peer,
            )
            copy.start()
            core_copies[b, k] = copy

    loads = [
        pltpu.make_async_copy(root_right, roots.at[:, span(y, c)], load_sem.at[0]),
        pltpu.make_async_copy(adam_second, second_v, load_sem.at[1]),
        pltpu.make_async_copy(root_left, root_v, load_sem.at[2]),
        pltpu.make_async_copy(weights, weights_v, load_sem.at[3]),
        pltpu.make_async_copy(stat_left, left_v, load_sem.at[4]),
        pltpu.make_async_copy(stat_right, right_v, load_sem.at[5]),
    ]
    for copy in loads:
        copy.start()

    def part_copy(q, k):
        return remote(
            part_out.at[q, k - 1],
            part_in.at[q, k - 1],
            part_s.at[q, k - 1],
            part_r.at[q, k - 1],
            replica(shifted(k), c),
        )

    def chip_sum(q, k):
        return own_rows[k, :, :, part(q)].astype(f32) + core_in[k, :, :, part(q)].astype(f32)

    for q in range(chunks):
        for k in range(1, outer):
            if q == 0:
                for b in range(per_index):
                    own_copies[b, k].wait()
                    core_copies[b, k].wait_recv()
            part_out[q, k - 1] = chip_sum(q, k).astype(bf16)
            part_copy(q, k).start()

    def far_copy(src, ref, s, k, sems):
        return remote(
            src, ref.at[s, span(y, c)], sems.at[0, s, k], sems.at[1, s, k], replica(shifted(k), c)
        )

    def near_copy(src, ref, s, k, sems):
        return remote(
            src, ref.at[s, span(back(k), c)], sems.at[2, s, k], sems.at[3, s, k], core_peer
        )

    def gather_start(src, ref, s, sems):
        for k in range(1, outer):
            far_copy(src, ref, s, k, sems).start()
        near_copy(src, ref, s, 0, sems).start()

    def gather_forward(ref, s, sems):
        for k in range(1, outer):
            landed = ref.at[s, span(back(k), c)]
            remote(landed, landed, sems.at[0, s, k], sems.at[1, s, k], core_peer).wait_recv()
            near_copy(landed, ref, s, k, sems).start()

    def gather_arrived(ref, s, sems):
        for k in range(outer):
            landed = ref.at[s, span(back(k), 1 - c)]
            remote(landed, landed, sems.at[2, s, k], sems.at[3, s, k], core_peer).wait_recv()

    def gather_sent(src, ref, s, sems):
        for k in range(1, outer):
            far_copy(src, ref, s, k, sems).wait_send()
        for k in range(outer):
            near_copy(src, ref, s, k, sems).wait_send()

    def slots(body):
        def step(s, carry):
            body(s)
            return carry

        lax.fori_loop(0, capacity, step, 0)

    loads[0].wait()
    slots(lambda s: gather_start(roots.at[s, span(y, c)], roots, s, root_sems))

    def send_up(src, d, q):
        return remote(
            blocks.at[src, q],
            blocks.at[src, q],
            up_s.at[d, q],
            block_r.at[src, q],
            group(o + 1, i),
        )

    def send_down(src, d, q):
        return remote(
            blocks.at[src, q],
            blocks.at[src, q],
            down_s.at[d, q],
            block_r.at[src, q],
            group(o - 1, i),
        )

    def wait_block(src, q):
        remote(
            blocks.at[src, q], blocks.at[src, q], up_s.at[0, q], block_r.at[src, q], cross_peer
        ).wait_recv()

    def cross_copy(src, q):
        return remote(
            cross_out.at[src, q],
            cross_in.at[src, q],
            cross_s.at[src, q],
            cross_r.at[src, q],
            cross_peer,
        )

    def cross(src, q):
        first = (src * PAIR + i) * per_index
        other = o * PAIR + 1 - i
        sent = blocks[src, q, 0]
        for b in range(1, per_index):
            sent = jnp.where(owner_ref[first + b] == other, blocks[src, q, b], sent)
        cross_out[src, q] = sent
        cross_copy(src, q).start()

    def own_total(q):
        if q == 0:
            for b in range(per_index):
                own_copies[b, 0].wait()
                core_copies[b, 0].wait_recv()
        total = chip_sum(q, 0)
        for k in range(1, outer):
            part_copy(q, k).wait_recv()
            total = total + part_in[q, k - 1].astype(f32)
        blocks[o, q] = total.astype(bf16)

        @pl.when(above)
        def _():
            send_up(o, 0, q).start()

        @pl.when(below)
        def _():
            send_down(o, 0, q).start()

        cross(o, q)

    def pass_on(d, q):
        @pl.when(o >= d)
        def _():
            wait_block(o - d, q)

            @pl.when(above)
            def _():
                send_up(o - d, d, q).start()

        @pl.when(o + d < layers)
        def _():
            wait_block(o + d, q)

            @pl.when(below)
            def _():
                send_down(o + d, d, q).start()

        @pl.when(o >= d)
        def _():
            cross(o - d, q)

        @pl.when(o + d < layers)
        def _():
            cross(o + d, q)

    def choose(q, s):
        found = jnp.int32(0)
        seen = jnp.int32(0)
        valid = jnp.int32(0)
        for b in range(count):
            hit = (owner_ref[b] == mine).astype(jnp.int32)
            take = hit * (seen == s).astype(jnp.int32)
            found = found + take * b
            valid = valid + take
            seen = seen + hit
        source = lax.div(found, per_index)
        layer, side = lax.div(source, PAIR), lax.rem(source, PAIR)
        within = lax.rem(found, per_index)
        crossed = jnp.zeros_like(cross_in[0, q])
        for src in range(layers):
            taken = cross_in[src, q]
            for b in range(per_index):
                straight = blocks[src, q, b]
                taken = jnp.where((side == i) & (within == b), straight, taken)
            crossed = jnp.where((layer == src) & (valid == 1), taken, crossed)
        f = q * capacity + s
        full[f, span(y, c)] = crossed
        gather_start(full.at[f, span(y, c)], full, f, grad_sems)

    def choose_chunk(q):
        for src in range(layers):
            cross_copy(src, q).wait_recv()
        slots(functools.partial(choose, q))

    for t in range(chunks + layers):
        if 0 <= t - layers < chunks:
            choose_chunk(t - layers)
        for d in range(layers - 1, 0, -1):
            if 0 <= t - d < chunks:
                pass_on(d, t - d)
        if t < chunks:
            own_total(t)

    for copy in loads[1:]:
        copy.wait()

    def store(ref, out, which, s):
        return pltpu.make_async_copy(ref.at[s], out.at[s], store_sem.at[which, s])

    row_of = lax.broadcasted_iota(jnp.int32, (8, 128), 0)

    def norm_copy(s, k):
        return remote(
            norm_out.at[s],
            norm_in.at[k - 1, s],
            norm_s.at[s, k - 1],
            norm_r.at[s, k - 1],
            {"dp": lax.rem(me + k, replicas), "own": mine},
        )

    def own_output(s):
        return pltpu.make_async_copy(
            fresh.at[s], out_weights.at[s, span(y, c)], store_sem.at[3, s]
        )

    def moments(s):
        adam_sq = jnp.float32(0)
        for q in range(chunks):
            grad32 = full[q * capacity + s, span(y, c)].astype(f32)
            second = 0.9 * second_v[s, :, part(q)] + 0.1 * grad32 * grad32
            second_v[s, :, part(q)] = second
            direction = grad32 / (jnp.sqrt(second) + 1e-08)
            adam_sq = adam_sq + jnp.sum(direction * direction)
        norm_out[s] = jnp.where(row_of < 4, adam_sq, 0.0)
        store(second_v, out_second, 0, s).start()

    def product(q, s):
        f = q * capacity + s
        gather_arrived(full, f, grad_sems)
        half = dot(root_v[s], full[f]).astype(bf16)
        return dot(half, roots[s, part(q), :])

    def accumulate(q, s):
        if q == 0:
            gather_arrived(roots, s, root_sems)
            precond[s] = product(q, s)
        else:
            precond[s] = precond[s] + product(q, s)

    def precondition(s):
        accumulate(chunks - 1, s)
        result = precond[s]
        norm_out[s] = norm_out[s] + jnp.where(row_of < 4, 0.0, jnp.sum(result * result))
        for k in range(1, replicas):
            norm_copy(s, k).start()

    def update(s):
        norms = norm_out[s]
        for k in range(1, replicas):
            norm_copy(s, k).wait_recv()
            norms = norms + norm_in[k - 1, s]
        graft = jnp.sqrt(norms[0:1, 0:1]) / (jnp.sqrt(norms[4:5, 0:1]) + 1e-06)
        fresh[s] = (weights_v[s] - graft * precond[s]).astype(bf16)
        gather_start(fresh.at[s], out_weights, s, weight_sems)
        own_output(s).start()

    slots(moments)
    slots(lambda s: gather_forward(roots, s, root_sems))
    for q in range(chunks - 1):
        slots(lambda s: gather_forward(full, q * capacity + s, grad_sems))
        slots(functools.partial(accumulate, q))

    def last(s, carry):
        @pl.when(s < capacity)
        def _():
            gather_forward(full, (chunks - 1) * capacity + s, grad_sems)

        @pl.when((s >= 1) & (s <= capacity))
        def _():
            precondition(s - 1)

        @pl.when(s >= 2)
        def _():
            update(s - 2)

        return carry

    lax.fori_loop(0, capacity + 2, last, 0)

    width = weights.shape[2]
    cols = width // replicas

    def pick(q):
        shape = (cols, CHUNK)
        column = lax.broadcasted_iota(jnp.int32, shape, 1) + q * CHUNK
        wanted = lax.broadcasted_iota(jnp.int32, shape, 0) + me * cols
        return (column == wanted).astype(f32).astype(bf16)

    def statistics(s):
        left, columns = 0.0, 0.0
        for q in range(chunks):
            f = q * capacity + s
            left = left + dot_nt(full[f, span(y, c)], full[f])
            columns = columns + dot_nt(pick(q), full[f])
        left_v[s] = 0.5 * left_v[s] + 0.5 * left
        store(left_v, out_left, 1, s).start()
        columns = columns.astype(bf16)
        for q in range(chunks):
            right_v[s, :, part(q)] = 0.5 * right_v[s, :, part(q)] + 0.5 * dot(
                columns, full[q * capacity + s]
            )
        store(right_v, out_right, 2, s).start()
        gather_forward(out_weights, s, weight_sems)

    slots(statistics)

    for copy in core_copies.values():
        copy.wait_send()
    for q in range(chunks):
        for k in range(1, outer):
            part_copy(q, k).wait_send()
        for d in range(layers - 1):

            @pl.when(above & (o >= d))
            def _():
                send_up(o - d, d, q).wait_send()

            @pl.when(below & (o + d < layers))
            def _():
                send_down(o + d, d, q).wait_send()

        for src in range(layers):
            cross_copy(src, q).wait_send()

    def finish(s):
        gather_sent(roots.at[s, span(y, c)], roots, s, root_sems)
        for q in range(chunks):
            f = q * capacity + s
            gather_sent(full.at[f, span(y, c)], full, f, grad_sems)
        for k in range(1, replicas):
            norm_copy(s, k).wait_send()
        store(second_v, out_second, 0, s).wait()
        store(left_v, out_left, 1, s).wait()
        store(right_v, out_right, 2, s).wait()
        own_output(s).wait()
        gather_arrived(out_weights, s, weight_sems)
        gather_sent(fresh.at[s], out_weights, s, weight_sems)

    slots(finish)


def write_out(*refs):
    sources, targets, sems = refs[:4], refs[4:8], refs[8]
    copies = [
        pltpu.make_async_copy(source.at[s], target.at[s], sems.at[n, s])
        for n, (source, target) in enumerate(zip(sources, targets))
        for s in range(source.shape[0])
    ]
    for copy in copies:
        copy.start()
    for copy in copies:
        copy.wait()


def on_device(
    replicas,
    owners,
    grads,
    owner,
    weights,
    stat_left,
    stat_right,
    adam_second,
    root_left,
    root_right,
):
    capacity, rows, width = weights.shape
    per_index, height = grads.shape[1], grads.shape[2]
    outer, layers = replicas // PAIR, owners // PAIR
    bf16, f32 = jnp.bfloat16, jnp.float32
    block, piece = (rows, width), (rows, CHUNK)
    chunks = width // CHUNK
    several = max(outer - 1, 1)
    dma = pltpu.SemaphoreType.DMA
    anywhere = pl.BlockSpec(memory_space=pl.ANY)
    scratch = [
        pltpu.VMEM((outer, per_index) + block, bf16),
        pltpu.VMEM((outer, per_index) + block, bf16),
        pltpu.VMEM((chunks, several, per_index) + piece, bf16),
        pltpu.VMEM((chunks, several, per_index) + piece, bf16),
        pltpu.VMEM((layers, chunks, per_index) + piece, bf16),
        pltpu.VMEM((layers, chunks) + piece, bf16),
        pltpu.VMEM((layers, chunks) + piece, bf16),
        pltpu.VMEM((chunks * capacity, height, CHUNK), bf16),
        pltpu.VMEM((capacity, width, width), bf16),
        pltpu.VMEM(stat_left.shape, f32),
        pltpu.VMEM(stat_right.shape, f32),
        pltpu.VMEM(adam_second.shape, f32),
        pltpu.VMEM(weights.shape, f32),
        pltpu.VMEM(root_left.shape, bf16),
        pltpu.VMEM(weights.shape, f32),
        pltpu.VMEM(weights.shape, bf16),
        pltpu.VMEM((capacity, 8, 128), f32),
        pltpu.VMEM((replicas - 1, capacity, 8, 128), f32),
        dma((6,)),
        dma((per_index, outer)),
        dma((4, capacity)),
        dma((per_index, outer)),
        dma((per_index, outer)),
        dma((chunks, several)),
        dma((chunks, several)),
        dma((layers, chunks)),
        dma((layers, chunks)),
        dma((layers, chunks)),
        dma((layers, chunks)),
        dma((layers, chunks)),
        dma((4, chunks * capacity, outer)),
        dma((4, capacity, outer)),
        dma((4, capacity, outer)),
        dma((capacity, replicas - 1)),
        dma((capacity, replicas - 1)),
    ]
    products = 5 * 2 * capacity * rows * width * width
    moved = 2 * grads.size + 32 * weights.size + 2 * capacity * height * width
    results = (
        ((capacity, height, width), bf16),
        (stat_left.shape, f32),
        (stat_right.shape, f32),
        (adam_second.shape, f32),
    )
    arrays = [
        pltpu.with_memory_space_constraint(array, pltpu.HBM)
        for array in (
            grads, weights, stat_left, stat_right, adam_second, root_left, root_right
        )
    ]
    near = pl.pallas_call(
        functools.partial(kernel, replicas, owners),
        out_shape=tuple(pltpu.VMEM(shape, dtype) for shape, dtype in results),
        in_specs=[pl.BlockSpec(memory_space=pltpu.SMEM)] + [anywhere] * 7,
        out_specs=(anywhere,) * 4,
        scratch_shapes=scratch,
        cost_estimate=pl.CostEstimate(
            flops=products, bytes_accessed=moved, transcendentals=weights.size
        ),
        compiler_params=pltpu.CompilerParams(
            collective_id=0, has_side_effects=True, vmem_limit_bytes=42 * 1024 * 1024
        ),
    )(owner, *arrays)
    return pl.pallas_call(
        write_out,
        out_shape=tuple(pltpu.HBM(shape, dtype) for shape, dtype in results),
        in_specs=[anywhere] * 4,
        out_specs=(anywhere,) * 4,
        scratch_shapes=[dma((4, capacity))],
    )(*near)


def solution(mesh):
    placed = (
        P("dp", "own", None, None),
        P(),
        P("own", "dp", None),
        P("own", "dp", None),
        P("own", "dp", None),
        P("own", "dp", None),
        P("own", "dp", None),
        P("own", "dp", None),
    )
    return jax.shard_map(
        functools.partial(on_device, mesh.shape["dp"], mesh.shape["own"]),
        mesh=mesh,
        in_specs=placed,
        out_specs=(
            P("own", None, None),
            P("own", "dp", None),
            P("own", "dp", None),
            P("own", "dp", None),
        ),
        check_vma=False,
    )
```

```python
import functools

import jax
import jax.numpy as jnp
from jax import lax
from jax.experimental import pallas as pl
from jax.experimental.pallas import tpu as pltpu
from jax.sharding import PartitionSpec as P

MESH = pl.DeviceIdType.MESH
PAIR = 2
CHUNK = 256


def dot(a, b):
    return lax.dot_general(a, b, (((1,), (0,)), ((), ())), preferred_element_type=jnp.float32)


def dot_nt(a, b):
    return lax.dot_general(a, b, (((1,), (1,)), ((), ())), preferred_element_type=jnp.float32)


def kernel(
    replicas,
    owners,
    owner_ref,
    grads,
    weights,
    stat_left,
    stat_right,
    adam_second,
    root_left,
    root_right,
    out_weights,
    out_left,
    out_right,
    out_second,
    own_rows,
    core_in,
    part_out,
    part_in,
    blocks,
    cross_out,
    cross_in,
    full,
    roots,
    left_v,
    right_v,
    second_v,
    weights_v,
    root_v,
    precond,
    fresh,
    norm_out,
    norm_in,
    load_sem,
    own_sem,
    store_sem,
    core_s,
    core_r,
    part_s,
    part_r,
    up_s,
    down_s,
    block_r,
    cross_s,
    cross_r,
    grad_sems,
    root_sems,
    weight_sems,
    norm_s,
    norm_r,
):
    outer = replicas // PAIR
    layers = owners // PAIR
    per_index = grads.shape[1]
    count = per_index * owners
    capacity = weights.shape[0]
    rows = weights.shape[1]
    chunks = weights.shape[2] // CHUNK
    me = lax.axis_index("dp")
    mine = lax.axis_index("own")
    y, c = lax.div(me, PAIR), lax.rem(me, PAIR)
    o, i = lax.div(mine, PAIR), lax.rem(mine, PAIR)
    f32, bf16 = jnp.float32, jnp.bfloat16

    def replica(yy, cc):
        return {"dp": yy * PAIR + cc, "own": mine}

    def group(oo, ii):
        return {"dp": me, "own": oo * PAIR + ii}

    def span(yy, cc):
        return pl.ds(pl.multiple_of((yy * PAIR + cc) * rows, rows), rows)

    def part(q):
        return pl.ds(q * CHUNK, CHUNK)

    def shifted(k):
        return lax.rem(y + k, outer)

    def back(k):
        return lax.rem(y + outer - k, outer)

    def remote(src, dst, send, recv, device):
        return pltpu.make_async_remote_copy(
            src_ref=src,
            dst_ref=dst,
            send_sem=send,
            recv_sem=recv,
            device_id=device,
            device_id_type=MESH,
        )

    core_peer = replica(y, 1 - c)
    cross_peer = group(o, 1 - i)
    above, below = o + 1 < layers, o >= 1

    own_copies = {}
    for b in range(per_index):
        for k in range(outer):
            copy = pltpu.make_async_copy(
                grads.at[0, b, span(shifted(k), c)], own_rows.at[k, b], own_sem.at[b, k]
            )
            copy.start()
            own_copies[b, k] = copy

    barrier = pltpu.get_barrier_semaphore()
    for k in range(1, replicas):
        pl.semaphore_signal(
            barrier,
            inc=1,
            device_id={"dp": lax.rem(me + k, replicas), "own": mine},
            device_id_type=MESH,
        )
    pl.semaphore_signal(barrier, inc=1, device_id=cross_peer, device_id_type=MESH)

    @pl.when(above)
    def _():
        pl.semaphore_signal(barrier, inc=1, device_id=group(o + 1, i), device_id_type=MESH)

    @pl.when(below)
    def _():
        pl.semaphore_signal(barrier, inc=1, device_id=group(o - 1, i), device_id_type=MESH)

    lines = above.astype(jnp.int32) + below.astype(jnp.int32)
    pl.semaphore_wait(barrier, replicas + lines)

    def far_copy(src, ref, s, k, sems):
        return remote(
            src, ref.at[s, span(y, c)], sems.at[0, s, k], sems.at[1, s, k], replica(shifted(k), c)
        )

    def near_copy(src, ref, s, k, sems):
        return remote(
            src, ref.at[s, span(back(k), c)], sems.at[2, s, k], sems.at[3, s, k], core_peer
        )

    def gather_start(src, ref, s, sems):
        for k in range(1, outer):
            far_copy(src, ref, s, k, sems).start()
        near_copy(src, ref, s, 0, sems).start()

    def gather_forward(ref, s, sems):
        for k in range(1, outer):
            landed = ref.at[s, span(back(k), c)]
            remote(landed, landed, sems.at[0, s, k], sems.at[1, s, k], core_peer).wait_recv()
            near_copy(landed, ref, s, k, sems).start()

    def gather_arrived(ref, s, sems):
        for k in range(outer):
            landed = ref.at[s, span(back(k), 1 - c)]
            remote(landed, landed, sems.at[2, s, k], sems.at[3, s, k], core_peer).wait_recv()

    def gather_sent(src, ref, s, sems):
        for k in range(1, outer):
            far_copy(src, ref, s, k, sems).wait_send()
        for k in range(outer):
            near_copy(src, ref, s, k, sems).wait_send()

    late = capacity - 1

    def roots_start(s):
        gather_start(root_right.at[s], roots, s, root_sems)

    roots_start(0)

    order = list(range(1, outer)) + [0]
    core_copies = {}
    for k in order:
        for b in range(per_index):
            copy = remote(
                grads.at[0, b, span(shifted(k), 1 - c)],
                core_in.at[k, b],
                core_s.at[b, k],
                core_r.at[b, k],
                core_peer,
            )
            copy.start()
            core_copies[b, k] = copy

    loads = [
        pltpu.make_async_copy(root_right, roots.at[:, span(y, c)], load_sem.at[0]),
        pltpu.make_async_copy(adam_second, second_v, load_sem.at[1]),
        pltpu.make_async_copy(root_left, root_v, load_sem.at[2]),
        pltpu.make_async_copy(weights, weights_v, load_sem.at[3]),
        pltpu.make_async_copy(stat_left, left_v, load_sem.at[4]),
        pltpu.make_async_copy(stat_right, right_v, load_sem.at[5]),
    ]
    for copy in loads:
        copy.start()

    def part_copy(q, k):
        return remote(
            part_out.at[q, k - 1],
            part_in.at[q, k - 1],
            part_s.at[q, k - 1],
            part_r.at[q, k - 1],
            replica(shifted(k), c),
        )

    def chip_sum(q, k):
        return own_rows[k, :, :, part(q)].astype(f32) + core_in[k, :, :, part(q)].astype(f32)

    for q in range(chunks):
        for k in range(1, outer):
            if q == 0:
                for b in range(per_index):
                    own_copies[b, k].wait()
                    core_copies[b, k].wait_recv()
            part_out[q, k - 1] = chip_sum(q, k).astype(bf16)
            part_copy(q, k).start()

    def slots(body):
        def step(s, carry):
            body(s)
            return carry

        lax.fori_loop(0, capacity, step, 0)

    for s in range(1, late):
        roots_start(s)

    def send_up(src, d, q):
        return remote(
            blocks.at[src, q],
            blocks.at[src, q],
            up_s.at[d, q],
            block_r.at[src, q],
            group(o + 1, i),
        )

    def send_down(src, d, q):
        return remote(
            blocks.at[src, q],
            blocks.at[src, q],
            down_s.at[d, q],
            block_r.at[src, q],
            group(o - 1, i),
        )

    def wait_block(src, q):
        remote(
            blocks.at[src, q], blocks.at[src, q], up_s.at[0, q], block_r.at[src, q], cross_peer
        ).wait_recv()

    def cross_copy(src, q):
        return remote(
            cross_out.at[src, q],
            cross_in.at[src, q],
            cross_s.at[src, q],
            cross_r.at[src, q],
            cross_peer,
        )

    def cross(src, q):
        first = (src * PAIR + i) * per_index
        other = o * PAIR + 1 - i
        sent = blocks[src, q, 0]
        for b in range(1, per_index):
            sent = jnp.where(owner_ref[first + b] == other, blocks[src, q, b], sent)
        cross_out[src, q] = sent
        cross_copy(src, q).start()

    def own_total(q):
        if q == 0:
            for b in range(per_index):
                own_copies[b, 0].wait()
                core_copies[b, 0].wait_recv()
        total = chip_sum(q, 0)
        for k in range(1, outer):
            part_copy(q, k).wait_recv()
            total = total + part_in[q, k - 1].astype(f32)
        blocks[o, q] = total.astype(bf16)

        @pl.when(above)
        def _():
            send_up(o, 0, q).start()

        @pl.when(below)
        def _():
            send_down(o, 0, q).start()

        cross(o, q)

    def pass_on(d, q):
        @pl.when(o >= d)
        def _():
            wait_block(o - d, q)

            @pl.when(above)
            def _():
                send_up(o - d, d, q).start()

        @pl.when(o + d < layers)
        def _():
            wait_block(o + d, q)

            @pl.when(below)
            def _():
                send_down(o + d, d, q).start()

        @pl.when(o >= d)
        def _():
            cross(o - d, q)

        @pl.when(o + d < layers)
        def _():
            cross(o + d, q)

    def choose(q, s):
        found = jnp.int32(0)
        seen = jnp.int32(0)
        valid = jnp.int32(0)
        for b in range(count):
            hit = (owner_ref[b] == mine).astype(jnp.int32)
            take = hit * (seen == s).astype(jnp.int32)
            found = found + take * b
            valid = valid + take
            seen = seen + hit
        source = lax.div(found, per_index)
        layer, side = lax.div(source, PAIR), lax.rem(source, PAIR)
        within = lax.rem(found, per_index)
        crossed = jnp.zeros_like(cross_in[0, q])
        for src in range(layers):
            taken = cross_in[src, q]
            for b in range(per_index):
                straight = blocks[src, q, b]
                taken = jnp.where((side == i) & (within == b), straight, taken)
            crossed = jnp.where((layer == src) & (valid == 1), taken, crossed)
        f = q * capacity + s
        full[f, span(y, c)] = crossed
        gather_start(full.at[f, span(y, c)], full, f, grad_sems)

    def choose_chunk(q):
        for src in range(layers):
            cross_copy(src, q).wait_recv()
        slots(functools.partial(choose, q))

    for t in range(chunks + layers):
        if 0 <= t - layers < chunks:
            choose_chunk(t - layers)
        for d in range(layers - 1, 0, -1):
            if 0 <= t - d < chunks:
                pass_on(d, t - d)
        if t < chunks:
            own_total(t)

    for copy in loads:
        copy.wait()

    def store(ref, out, which, s):
        return pltpu.make_async_copy(ref.at[s], out.at[s], store_sem.at[which, s])

    row_of = lax.broadcasted_iota(jnp.int32, (8, 128), 0)

    def norm_copy(s, k):
        return remote(
            norm_out.at[s],
            norm_in.at[k - 1, s],
            norm_s.at[s, k - 1],
            norm_r.at[s, k - 1],
            {"dp": lax.rem(me + k, replicas), "own": mine},
        )

    def own_output(s):
        return pltpu.make_async_copy(
            fresh.at[s], out_weights.at[s, span(y, c)], store_sem.at[3, s]
        )

    def moments(s):
        adam_sq = jnp.float32(0)
        for q in range(chunks):
            grad32 = full[q * capacity + s, span(y, c)].astype(f32)
            second = 0.9 * second_v[s, :, part(q)] + 0.1 * grad32 * grad32
            second_v[s, :, part(q)] = second
            direction = grad32 / (jnp.sqrt(second) + 1e-08)
            adam_sq = adam_sq + jnp.sum(direction * direction)
        norm_out[s] = jnp.where(row_of < 4, adam_sq, 0.0)
        store(second_v, out_second, 0, s).start()

    def product(q, s):
        f = q * capacity + s
        gather_arrived(full, f, grad_sems)
        half = dot(root_v[s], full[f]).astype(bf16)
        return dot(half, roots[s, part(q), :])

    def accumulate(q, s):
        if q == 0:
            gather_arrived(roots, s, root_sems)
            precond[s] = product(q, s)
        else:
            precond[s] = precond[s] + product(q, s)

    def precondition(s):
        accumulate(chunks - 1, s)
        result = precond[s]
        norm_out[s] = norm_out[s] + jnp.where(row_of < 4, 0.0, jnp.sum(result * result))
        for k in range(1, replicas):
            norm_copy(s, k).start()

    def update(s):
        norms = norm_out[s]
        for k in range(1, replicas):
            norm_copy(s, k).wait_recv()
            norms = norms + norm_in[k - 1, s]
        graft = jnp.sqrt(norms[0:1, 0:1]) / (jnp.sqrt(norms[4:5, 0:1]) + 1e-06)
        fresh[s] = (weights_v[s] - graft * precond[s]).astype(bf16)
        gather_start(fresh.at[s], out_weights, s, weight_sems)
        own_output(s).start()

    def early(body):
        def step(s, carry):
            body(s)
            return carry

        lax.fori_loop(0, late, step, 0)

    slots(moments)
    early(lambda s: gather_forward(roots, s, root_sems))
    for q in range(chunks - 1):
        slots(lambda s: gather_forward(full, q * capacity + s, grad_sems))
        early(functools.partial(accumulate, q))

    def last(s, carry):
        gather_forward(full, (chunks - 1) * capacity + s, grad_sems)

        @pl.when(s >= 1)
        def _():
            precondition(s - 1)

        @pl.when(s == 1)
        def _():
            roots_start(late)

        @pl.when(s >= 2)
        def _():
            update(s - 2)

        return carry

    lax.fori_loop(0, capacity, last, 0)
    gather_forward(roots, late, root_sems)
    for q in range(chunks - 1):
        accumulate(q, late)
    precondition(late)
    update(late - 1)

    width = weights.shape[2]
    cols = width // replicas

    def pick(q):
        shape = (cols, CHUNK)
        column = lax.broadcasted_iota(jnp.int32, shape, 1) + q * CHUNK
        wanted = lax.broadcasted_iota(jnp.int32, shape, 0) + me * cols
        return (column == wanted).astype(f32).astype(bf16)

    def statistics(s):
        left, columns = 0.0, 0.0
        for q in range(chunks):
            f = q * capacity + s
            left = left + dot_nt(full[f, span(y, c)], full[f])
            columns = columns + dot_nt(pick(q), full[f])
        left_v[s] = 0.5 * left_v[s] + 0.5 * left
        store(left_v, out_left, 1, s).start()
        columns = columns.astype(bf16)
        for q in range(chunks):
            right_v[s, :, part(q)] = 0.5 * right_v[s, :, part(q)] + 0.5 * dot(
                columns, full[q * capacity + s]
            )
        store(right_v, out_right, 2, s).start()

    slots(statistics)
    gather_forward(out_weights, 0, weight_sems)
    update(late)
    for s in range(1, capacity):
        gather_forward(out_weights, s, weight_sems)

    for copy in core_copies.values():
        copy.wait_send()
    for q in range(chunks):
        for k in range(1, outer):
            part_copy(q, k).wait_send()
        for d in range(layers - 1):

            @pl.when(above & (o >= d))
            def _():
                send_up(o - d, d, q).wait_send()

            @pl.when(below & (o + d < layers))
            def _():
                send_down(o + d, d, q).wait_send()

        for src in range(layers):
            cross_copy(src, q).wait_send()

    def finish(s):
        gather_sent(roots.at[s, span(y, c)], roots, s, root_sems)
        for q in range(chunks):
            f = q * capacity + s
            gather_sent(full.at[f, span(y, c)], full, f, grad_sems)
        for k in range(1, replicas):
            norm_copy(s, k).wait_send()
        store(second_v, out_second, 0, s).wait()
        store(left_v, out_left, 1, s).wait()
        store(right_v, out_right, 2, s).wait()
        own_output(s).wait()
        gather_arrived(out_weights, s, weight_sems)
        gather_sent(fresh.at[s], out_weights, s, weight_sems)

    slots(finish)


def write_out(*refs):
    sources, targets, sems = refs[:4], refs[4:8], refs[8]
    copies = [
        pltpu.make_async_copy(source.at[s], target.at[s], sems.at[n, s])
        for n, (source, target) in enumerate(zip(sources, targets))
        for s in range(source.shape[0])
    ]
    for copy in copies:
        copy.start()
    for copy in copies:
        copy.wait()


def on_device(
    replicas,
    owners,
    grads,
    owner,
    weights,
    stat_left,
    stat_right,
    adam_second,
    root_left,
    root_right,
):
    capacity, rows, width = weights.shape
    per_index, height = grads.shape[1], grads.shape[2]
    outer, layers = replicas // PAIR, owners // PAIR
    bf16, f32 = jnp.bfloat16, jnp.float32
    block, piece = (rows, width), (rows, CHUNK)
    chunks = width // CHUNK
    several = max(outer - 1, 1)
    dma = pltpu.SemaphoreType.DMA
    anywhere = pl.BlockSpec(memory_space=pl.ANY)
    scratch = [
        pltpu.VMEM((outer, per_index) + block, bf16),
        pltpu.VMEM((outer, per_index) + block, bf16),
        pltpu.VMEM((chunks, several, per_index) + piece, bf16),
        pltpu.VMEM((chunks, several, per_index) + piece, bf16),
        pltpu.VMEM((layers, chunks, per_index) + piece, bf16),
        pltpu.VMEM((layers, chunks) + piece, bf16),
        pltpu.VMEM((layers, chunks) + piece, bf16),
        pltpu.VMEM((chunks * capacity, height, CHUNK), bf16),
        pltpu.VMEM((capacity, width, width), bf16),
        pltpu.VMEM(stat_left.shape, f32),
        pltpu.VMEM(stat_right.shape, f32),
        pltpu.VMEM(adam_second.shape, f32),
        pltpu.VMEM(weights.shape, f32),
        pltpu.VMEM(root_left.shape, bf16),
        pltpu.VMEM(weights.shape, f32),
        pltpu.VMEM(weights.shape, bf16),
        pltpu.VMEM((capacity, 8, 128), f32),
        pltpu.VMEM((replicas - 1, capacity, 8, 128), f32),
        dma((6,)),
        dma((per_index, outer)),
        dma((4, capacity)),
        dma((per_index, outer)),
        dma((per_index, outer)),
        dma((chunks, several)),
        dma((chunks, several)),
        dma((layers, chunks)),
        dma((layers, chunks)),
        dma((layers, chunks)),
        dma((layers, chunks)),
        dma((layers, chunks)),
        dma((4, chunks * capacity, outer)),
        dma((4, capacity, outer)),
        dma((4, capacity, outer)),
        dma((capacity, replicas - 1)),
        dma((capacity, replicas - 1)),
    ]
    products = 5 * 2 * capacity * rows * width * width
    moved = 2 * grads.size + 32 * weights.size + 2 * capacity * height * width
    results = (
        ((capacity, height, width), bf16),
        (stat_left.shape, f32),
        (stat_right.shape, f32),
        (adam_second.shape, f32),
    )
    arrays = [
        pltpu.with_memory_space_constraint(array, pltpu.HBM)
        for array in (
            grads, weights, stat_left, stat_right, adam_second, root_left, root_right
        )
    ]
    near = pl.pallas_call(
        functools.partial(kernel, replicas, owners),
        out_shape=tuple(pltpu.VMEM(shape, dtype) for shape, dtype in results),
        in_specs=[pl.BlockSpec(memory_space=pltpu.SMEM)] + [anywhere] * 7,
        out_specs=(anywhere,) * 4,
        scratch_shapes=scratch,
        cost_estimate=pl.CostEstimate(
            flops=products, bytes_accessed=moved, transcendentals=weights.size
        ),
        compiler_params=pltpu.CompilerParams(
            collective_id=0, has_side_effects=True, vmem_limit_bytes=42 * 1024 * 1024
        ),
    )(pltpu.with_memory_space_constraint(owner, pltpu.HBM), *arrays)
    return pl.pallas_call(
        write_out,
        out_shape=tuple(pltpu.HBM(shape, dtype) for shape, dtype in results),
        in_specs=[anywhere] * 4,
        out_specs=(anywhere,) * 4,
        scratch_shapes=[dma((4, capacity))],
        compiler_params=pltpu.CompilerParams(vmem_limit_bytes=4 * 1024 * 1024),
    )(*[pltpu.with_memory_space_constraint(array, pltpu.VMEM) for array in near])


def solution(mesh):
    placed = (
        P("dp", "own", None, None),
        P(),
        P("own", "dp", None),
        P("own", "dp", None),
        P("own", "dp", None),
        P("own", "dp", None),
        P("own", "dp", None),
        P("own", "dp", None),
    )
    return jax.shard_map(
        functools.partial(on_device, mesh.shape["dp"], mesh.shape["own"]),
        mesh=mesh,
        in_specs=placed,
        out_specs=(
            P("own", None, None),
            P("own", "dp", None),
            P("own", "dp", None),
            P("own", "dp", None),
        ),
        check_vma=False,
    )
```

```python
import functools

import jax
import jax.numpy as jnp
from jax import lax
from jax.experimental import pallas as pl
from jax.experimental.pallas import tpu as pltpu
from jax.sharding import PartitionSpec as P

MESH = pl.DeviceIdType.MESH
PAIR = 2
CHUNK = 128


def dot(a, b):
    return lax.dot_general(a, b, (((1,), (0,)), ((), ())), preferred_element_type=jnp.float32)


def dot_nt(a, b):
    return lax.dot_general(a, b, (((1,), (1,)), ((), ())), preferred_element_type=jnp.float32)


def kernel(
    replicas,
    owners,
    owner_ref,
    grads,
    weights,
    stat_left,
    stat_right,
    adam_second,
    root_left,
    root_right,
    out_weights,
    out_left,
    out_right,
    out_second,
    own_rows,
    core_in,
    part_out,
    part_in,
    blocks,
    cross_out,
    cross_in,
    full,
    roots,
    left_v,
    right_v,
    second_v,
    weights_v,
    root_v,
    precond,
    fresh,
    norm_out,
    norm_in,
    load_sem,
    own_sem,
    store_sem,
    core_s,
    core_r,
    part_s,
    part_r,
    up_s,
    down_s,
    block_r,
    cross_s,
    cross_r,
    grad_sems,
    root_sems,
    weight_sems,
    norm_s,
    norm_r,
):
    outer = replicas // PAIR
    layers = owners // PAIR
    per_index = grads.shape[1]
    count = per_index * owners
    capacity = weights.shape[0]
    rows = weights.shape[1]
    chunks = weights.shape[2] // CHUNK
    me = lax.axis_index("dp")
    mine = lax.axis_index("own")
    y, c = lax.div(me, PAIR), lax.rem(me, PAIR)
    o, i = lax.div(mine, PAIR), lax.rem(mine, PAIR)
    f32, bf16 = jnp.float32, jnp.bfloat16

    def replica(yy, cc):
        return {"dp": yy * PAIR + cc, "own": mine}

    def group(oo, ii):
        return {"dp": me, "own": oo * PAIR + ii}

    def span(yy, cc):
        return pl.ds(pl.multiple_of((yy * PAIR + cc) * rows, rows), rows)

    def part(q):
        return pl.ds(q * CHUNK, CHUNK)

    def shifted(k):
        return lax.rem(y + k, outer)

    def back(k):
        return lax.rem(y + outer - k, outer)

    def remote(src, dst, send, recv, device):
        return pltpu.make_async_remote_copy(
            src_ref=src,
            dst_ref=dst,
            send_sem=send,
            recv_sem=recv,
            device_id=device,
            device_id_type=MESH,
        )

    core_peer = replica(y, 1 - c)
    cross_peer = group(o, 1 - i)
    above, below = o + 1 < layers, o >= 1

    own_copies = {}
    for b in range(per_index):
        for k in range(outer):
            copy = pltpu.make_async_copy(
                grads.at[0, b, span(shifted(k), c)], own_rows.at[k, b], own_sem.at[b, k]
            )
            copy.start()
            own_copies[b, k] = copy

    barrier = pltpu.get_barrier_semaphore()
    for k in range(1, replicas):
        pl.semaphore_signal(
            barrier,
            inc=1,
            device_id={"dp": lax.rem(me + k, replicas), "own": mine},
            device_id_type=MESH,
        )
    pl.semaphore_signal(barrier, inc=1, device_id=cross_peer, device_id_type=MESH)

    @pl.when(above)
    def _():
        pl.semaphore_signal(barrier, inc=1, device_id=group(o + 1, i), device_id_type=MESH)

    @pl.when(below)
    def _():
        pl.semaphore_signal(barrier, inc=1, device_id=group(o - 1, i), device_id_type=MESH)

    lines = above.astype(jnp.int32) + below.astype(jnp.int32)
    pl.semaphore_wait(barrier, replicas + lines)

    def far_copy(src, ref, s, k, sems):
        return remote(
            src, ref.at[s, span(y, c)], sems.at[0, s, k], sems.at[1, s, k], replica(shifted(k), c)
        )

    def near_copy(src, ref, s, k, sems):
        return remote(
            src, ref.at[s, span(back(k), c)], sems.at[2, s, k], sems.at[3, s, k], core_peer
        )

    def gather_start(src, ref, s, sems):
        for k in range(1, outer):
            far_copy(src, ref, s, k, sems).start()
        near_copy(src, ref, s, 0, sems).start()

    def gather_forward(ref, s, sems):
        for k in range(1, outer):
            landed = ref.at[s, span(back(k), c)]
            remote(landed, landed, sems.at[0, s, k], sems.at[1, s, k], core_peer).wait_recv()
            near_copy(landed, ref, s, k, sems).start()

    def gather_arrived(ref, s, sems):
        for k in range(outer):
            landed = ref.at[s, span(back(k), 1 - c)]
            remote(landed, landed, sems.at[2, s, k], sems.at[3, s, k], core_peer).wait_recv()

    def gather_sent(src, ref, s, sems):
        for k in range(1, outer):
            far_copy(src, ref, s, k, sems).wait_send()
        for k in range(outer):
            near_copy(src, ref, s, k, sems).wait_send()

    order = list(range(1, outer)) + [0]
    core_copies = {}
    for k in order:
        for b in range(per_index):
            copy = remote(
                grads.at[0, b, span(shifted(k), 1 - c)],
                core_in.at[k, b],
                core_s.at[b, k],
                core_r.at[b, k],
                core_peer,
            )
            copy.start()
            core_copies[b, k] = copy

    loads = [
        pltpu.make_async_copy(root_right, roots.at[:, span(y, c)], load_sem.at[0]),
        pltpu.make_async_copy(adam_second, second_v, load_sem.at[1]),
        pltpu.make_async_copy(root_left, root_v, load_sem.at[2]),
        pltpu.make_async_copy(weights, weights_v, load_sem.at[3]),
        pltpu.make_async_copy(stat_left, left_v, load_sem.at[4]),
        pltpu.make_async_copy(stat_right, right_v, load_sem.at[5]),
    ]
    for copy in loads:
        copy.start()

    def part_copy(q, k):
        return remote(
            part_out.at[q, k - 1],
            part_in.at[q, k - 1],
            part_s.at[q, k - 1],
            part_r.at[q, k - 1],
            replica(shifted(k), c),
        )

    def chip_sum(q, k):
        return own_rows[k, :, :, part(q)].astype(f32) + core_in[k, :, :, part(q)].astype(f32)

    for q in range(chunks):
        for k in range(1, outer):
            if q == 0:
                for b in range(per_index):
                    own_copies[b, k].wait()
                    core_copies[b, k].wait_recv()
            part_out[q, k - 1] = chip_sum(q, k).astype(bf16)
            part_copy(q, k).start()

    def slots(body):
        def step(s, carry):
            body(s)
            return carry

        lax.fori_loop(0, capacity, step, 0)

    slots(lambda s: gather_start(root_right.at[s], roots, s, root_sems))

    def send_up(src, d, q):
        return remote(
            blocks.at[src, q],
            blocks.at[src, q],
            up_s.at[d, q],
            block_r.at[src, q],
            group(o + 1, i),
        )

    def send_down(src, d, q):
        return remote(
            blocks.at[src, q],
            blocks.at[src, q],
            down_s.at[d, q],
            block_r.at[src, q],
            group(o - 1, i),
        )

    def wait_block(src, q):
        remote(
            blocks.at[src, q], blocks.at[src, q], up_s.at[0, q], block_r.at[src, q], cross_peer
        ).wait_recv()

    def cross_copy(src, q):
        return remote(
            cross_out.at[src, q],
            cross_in.at[src, q],
            cross_s.at[src, q],
            cross_r.at[src, q],
            cross_peer,
        )

    def cross(src, q):
        first = (src * PAIR + i) * per_index
        other = o * PAIR + 1 - i
        sent = blocks[src, q, 0]
        for b in range(1, per_index):
            sent = jnp.where(owner_ref[first + b] == other, blocks[src, q, b], sent)
        cross_out[src, q] = sent
        cross_copy(src, q).start()

    def own_total(q):
        if q == 0:
            for b in range(per_index):
                own_copies[b, 0].wait()
                core_copies[b, 0].wait_recv()
        total = chip_sum(q, 0)
        for k in range(1, outer):
            part_copy(q, k).wait_recv()
            total = total + part_in[q, k - 1].astype(f32)
        blocks[o, q] = total.astype(bf16)

        @pl.when(above)
        def _():
            send_up(o, 0, q).start()

        @pl.when(below)
        def _():
            send_down(o, 0, q).start()

        cross(o, q)

    def pass_on(d, q):
        @pl.when(o >= d)
        def _():
            wait_block(o - d, q)

            @pl.when(above)
            def _():
                send_up(o - d, d, q).start()

        @pl.when(o + d < layers)
        def _():
            wait_block(o + d, q)

            @pl.when(below)
            def _():
                send_down(o + d, d, q).start()

        @pl.when(o >= d)
        def _():
            cross(o - d, q)

        @pl.when(o + d < layers)
        def _():
            cross(o + d, q)

    def choose(q, s):
        found = jnp.int32(0)
        seen = jnp.int32(0)
        valid = jnp.int32(0)
        for b in range(count):
            hit = (owner_ref[b] == mine).astype(jnp.int32)
            take = hit * (seen == s).astype(jnp.int32)
            found = found + take * b
            valid = valid + take
            seen = seen + hit
        source = lax.div(found, per_index)
        layer, side = lax.div(source, PAIR), lax.rem(source, PAIR)
        within = lax.rem(found, per_index)
        crossed = jnp.zeros_like(cross_in[0, q])
        for src in range(layers):
            taken = cross_in[src, q]
            for b in range(per_index):
                straight = blocks[src, q, b]
                taken = jnp.where((side == i) & (within == b), straight, taken)
            crossed = jnp.where((layer == src) & (valid == 1), taken, crossed)
        f = q * capacity + s
        full[f, span(y, c)] = crossed
        gather_start(full.at[f, span(y, c)], full, f, grad_sems)

    def choose_chunk(q):
        for src in range(layers):
            cross_copy(src, q).wait_recv()
        slots(functools.partial(choose, q))

    for t in range(chunks + layers):
        if 0 <= t - layers < chunks:
            choose_chunk(t - layers)
        for d in range(layers - 1, 0, -1):
            if 0 <= t - d < chunks:
                pass_on(d, t - d)
        if t < chunks:
            own_total(t)

    for copy in loads:
        copy.wait()

    def store(ref, out, which, s):
        return pltpu.make_async_copy(ref.at[s], out.at[s], store_sem.at[which, s])

    row_of = lax.broadcasted_iota(jnp.int32, (8, 128), 0)

    def norm_copy(s, k):
        return remote(
            norm_out.at[s],
            norm_in.at[k - 1, s],
            norm_s.at[s, k - 1],
            norm_r.at[s, k - 1],
            {"dp": lax.rem(me + k, replicas), "own": mine},
        )

    def own_output(s):
        return pltpu.make_async_copy(
            fresh.at[s], out_weights.at[s, span(y, c)], store_sem.at[3, s]
        )

    def moments(s):
        adam_sq = jnp.float32(0)
        for q in range(chunks):
            grad32 = full[q * capacity + s, span(y, c)].astype(f32)
            second = 0.9 * second_v[s, :, part(q)] + 0.1 * grad32 * grad32
            second_v[s, :, part(q)] = second
            direction = grad32 / (jnp.sqrt(second) + 1e-08)
            adam_sq = adam_sq + jnp.sum(direction * direction)
        norm_out[s] = jnp.where(row_of < 4, adam_sq, 0.0)
        store(second_v, out_second, 0, s).start()

    def product(q, s):
        f = q * capacity + s
        gather_arrived(full, f, grad_sems)
        half = dot(root_v[s], full[f]).astype(bf16)
        return dot(half, roots[s, part(q), :])

    def accumulate(q, s):
        if q == 0:
            gather_arrived(roots, s, root_sems)
            precond[s] = product(q, s)
        else:
            precond[s] = precond[s] + product(q, s)

    def precondition(s):
        accumulate(chunks - 1, s)
        result = precond[s]
        norm_out[s] = norm_out[s] + jnp.where(row_of < 4, 0.0, jnp.sum(result * result))
        for k in range(1, replicas):
            norm_copy(s, k).start()

    def update(s):
        norms = norm_out[s]
        for k in range(1, replicas):
            norm_copy(s, k).wait_recv()
            norms = norms + norm_in[k - 1, s]
        graft = jnp.sqrt(norms[0:1, 0:1]) / (jnp.sqrt(norms[4:5, 0:1]) + 1e-06)
        fresh[s] = (weights_v[s] - graft * precond[s]).astype(bf16)
        gather_start(fresh.at[s], out_weights, s, weight_sems)
        own_output(s).start()

    slots(moments)
    slots(lambda s: gather_forward(roots, s, root_sems))
    for q in range(chunks - 1):
        slots(lambda s: gather_forward(full, q * capacity + s, grad_sems))
        slots(functools.partial(accumulate, q))

    def last(s, carry):
        @pl.when(s < capacity)
        def _():
            gather_forward(full, (chunks - 1) * capacity + s, grad_sems)

        @pl.when((s >= 1) & (s <= capacity))
        def _():
            precondition(s - 1)

        @pl.when(s >= 2)
        def _():
            update(s - 2)

        return carry

    lax.fori_loop(0, capacity + 2, last, 0)

    width = weights.shape[2]
    cols = width // replicas

    def pick(q):
        shape = (cols, CHUNK)
        column = lax.broadcasted_iota(jnp.int32, shape, 1) + q * CHUNK
        wanted = lax.broadcasted_iota(jnp.int32, shape, 0) + me * cols
        return (column == wanted).astype(f32).astype(bf16)

    def statistics(s):
        left, columns = 0.0, 0.0
        for q in range(chunks):
            f = q * capacity + s
            left = left + dot_nt(full[f, span(y, c)], full[f])
            columns = columns + dot_nt(pick(q), full[f])
        left_v[s] = 0.5 * left_v[s] + 0.5 * left
        store(left_v, out_left, 1, s).start()
        columns = columns.astype(bf16)
        for q in range(chunks):
            right_v[s, :, part(q)] = 0.5 * right_v[s, :, part(q)] + 0.5 * dot(
                columns, full[q * capacity + s]
            )
        store(right_v, out_right, 2, s).start()

    slots(statistics)
    slots(lambda s: gather_forward(out_weights, s, weight_sems))

    for copy in core_copies.values():
        copy.wait_send()
    for q in range(chunks):
        for k in range(1, outer):
            part_copy(q, k).wait_send()
        for d in range(layers - 1):

            @pl.when(above & (o >= d))
            def _():
                send_up(o - d, d, q).wait_send()

            @pl.when(below & (o + d < layers))
            def _():
                send_down(o + d, d, q).wait_send()

        for src in range(layers):
            cross_copy(src, q).wait_send()

    def finish(s):
        gather_sent(roots.at[s, span(y, c)], roots, s, root_sems)
        for q in range(chunks):
            f = q * capacity + s
            gather_sent(full.at[f, span(y, c)], full, f, grad_sems)
        for k in range(1, replicas):
            norm_copy(s, k).wait_send()
        store(second_v, out_second, 0, s).wait()
        store(left_v, out_left, 1, s).wait()
        store(right_v, out_right, 2, s).wait()
        own_output(s).wait()
        gather_arrived(out_weights, s, weight_sems)
        gather_sent(fresh.at[s], out_weights, s, weight_sems)

    slots(finish)


def write_out(*refs):
    sources, targets, sems = refs[:4], refs[4:8], refs[8]
    copies = [
        pltpu.make_async_copy(source.at[s], target.at[s], sems.at[n, s])
        for n, (source, target) in enumerate(zip(sources, targets))
        for s in range(source.shape[0])
    ]
    for copy in copies:
        copy.start()
    for copy in copies:
        copy.wait()


def on_device(
    replicas,
    owners,
    grads,
    owner,
    weights,
    stat_left,
    stat_right,
    adam_second,
    root_left,
    root_right,
):
    capacity, rows, width = weights.shape
    per_index, height = grads.shape[1], grads.shape[2]
    outer, layers = replicas // PAIR, owners // PAIR
    bf16, f32 = jnp.bfloat16, jnp.float32
    block, piece = (rows, width), (rows, CHUNK)
    chunks = width // CHUNK
    several = max(outer - 1, 1)
    dma = pltpu.SemaphoreType.DMA
    anywhere = pl.BlockSpec(memory_space=pl.ANY)
    scratch = [
        pltpu.VMEM((outer, per_index) + block, bf16),
        pltpu.VMEM((outer, per_index) + block, bf16),
        pltpu.VMEM((chunks, several, per_index) + piece, bf16),
        pltpu.VMEM((chunks, several, per_index) + piece, bf16),
        pltpu.VMEM((layers, chunks, per_index) + piece, bf16),
        pltpu.VMEM((layers, chunks) + piece, bf16),
        pltpu.VMEM((layers, chunks) + piece, bf16),
        pltpu.VMEM((chunks * capacity, height, CHUNK), bf16),
        pltpu.VMEM((capacity, width, width), bf16),
        pltpu.VMEM(stat_left.shape, f32),
        pltpu.VMEM(stat_right.shape, f32),
        pltpu.VMEM(adam_second.shape, f32),
        pltpu.VMEM(weights.shape, f32),
        pltpu.VMEM(root_left.shape, bf16),
        pltpu.VMEM(weights.shape, f32),
        pltpu.VMEM(weights.shape, bf16),
        pltpu.VMEM((capacity, 8, 128), f32),
        pltpu.VMEM((replicas - 1, capacity, 8, 128), f32),
        dma((6,)),
        dma((per_index, outer)),
        dma((4, capacity)),
        dma((per_index, outer)),
        dma((per_index, outer)),
        dma((chunks, several)),
        dma((chunks, several)),
        dma((layers, chunks)),
        dma((layers, chunks)),
        dma((layers, chunks)),
        dma((layers, chunks)),
        dma((layers, chunks)),
        dma((4, chunks * capacity, outer)),
        dma((4, capacity, outer)),
        dma((4, capacity, outer)),
        dma((capacity, replicas - 1)),
        dma((capacity, replicas - 1)),
    ]
    products = 5 * 2 * capacity * rows * width * width
    moved = 2 * grads.size + 32 * weights.size + 2 * capacity * height * width
    results = (
        ((capacity, height, width), bf16),
        (stat_left.shape, f32),
        (stat_right.shape, f32),
        (adam_second.shape, f32),
    )
    arrays = [
        pltpu.with_memory_space_constraint(array, pltpu.HBM)
        for array in (
            grads, weights, stat_left, stat_right, adam_second, root_left, root_right
        )
    ]
    near = pl.pallas_call(
        functools.partial(kernel, replicas, owners),
        out_shape=tuple(pltpu.VMEM(shape, dtype) for shape, dtype in results),
        in_specs=[pl.BlockSpec(memory_space=pltpu.SMEM)] + [anywhere] * 7,
        out_specs=(anywhere,) * 4,
        scratch_shapes=scratch,
        cost_estimate=pl.CostEstimate(
            flops=products, bytes_accessed=moved, transcendentals=weights.size
        ),
        compiler_params=pltpu.CompilerParams(
            collective_id=0, has_side_effects=True, vmem_limit_bytes=42 * 1024 * 1024
        ),
    )(pltpu.with_memory_space_constraint(owner, pltpu.HBM), *arrays)
    return pl.pallas_call(
        write_out,
        out_shape=tuple(pltpu.HBM(shape, dtype) for shape, dtype in results),
        in_specs=[anywhere] * 4,
        out_specs=(anywhere,) * 4,
        scratch_shapes=[dma((4, capacity))],
        compiler_params=pltpu.CompilerParams(vmem_limit_bytes=4 * 1024 * 1024),
    )(*[pltpu.with_memory_space_constraint(array, pltpu.VMEM) for array in near])


def solution(mesh):
    placed = (
        P("dp", "own", None, None),
        P(),
        P("own", "dp", None),
        P("own", "dp", None),
        P("own", "dp", None),
        P("own", "dp", None),
        P("own", "dp", None),
        P("own", "dp", None),
    )
    return jax.shard_map(
        functools.partial(on_device, mesh.shape["dp"], mesh.shape["own"]),
        mesh=mesh,
        in_specs=placed,
        out_specs=(
            P("own", None, None),
            P("own", "dp", None),
            P("own", "dp", None),
            P("own", "dp", None),
        ),
        check_vma=False,
    )
```
